512 devices in a mesh: cls: 64 (over x, y, core), dp: 8 (over z).
Axes of the slice: x: 4, y: 8, z: 8, core: 2. Of those that a mesh axis runs over, the one named last changes fastest.
Arguments:
- features: bfloat16 [65536, 4096], P(('cls', 'dp')), may hold values from -24 to 24
- proj: bfloat16 [4096, 128], replicated, may hold values from -0.09375 to 0.09375
- class_emb: bfloat16 [524288, 128], P('cls'), may hold values from -64 to 64
- lists: int32 [64, 8, 6], P(None, 'dp'), may hold values from -1 to 63, as said below
- labels: int32 [64, 8, 128], P(None, 'dp'), may hold values from 0 to 524287, as said below
Outputs:
- loss: float32 [65536], P(('cls', 'dp'))
- class_grad: float32 [524288, 128], P(('cls', 'dp'))
- proj_grad: float32 [4096, 128], P(('cls', 'dp'))
The draws below stay inside these ranges and needn't reach their ends.
Inputs may be any that keep to these rules, and one draw needn't show every extreme that they name: Each row block lists 1 to 6 distinct class blocks in the first entries of its row, -1 after. Within one group, each class block is listed by at most 6 row blocks, and in every group some class block is listed by exactly 6 of them. `labels`: each row's label lies in a class block that its row block lists.
All inputs are finite; a program needn't handle non-finite values.
Results may differ from the reference program's by a relative error of at most 0.014.
Values may be sent and summed in bfloat16 or wider, within the bound.
No kernel may reach another device: no remote copies, remote signals or barrier semaphores. Data moves between devices by JAX's collectives and lax.ppermute only.
A program may use at most 128 MiB of HBM per device.

```python
import jax
import jax.numpy as jnp
from jax import lax

D = 4096
R = 128
BLK = 8192
ROW_DEV = 128
LIST = 6
BLOCKS = 64
GROUPS = 8
ROWS = 65536
CLASSES = 524288


def list_table(key):
    base_key = jax.random.fold_in(key, 5)

    def one_group(group_key):
        keys = jax.random.split(group_key, 5)
        placed = jax.random.permutation(keys[0], BLOCKS)
        blocks_in_order = jax.random.permutation(keys[1], BLOCKS)
        first_draw = jax.random.randint(keys[2], (BLOCKS,), 0, 6)
        second_draw = jax.random.randint(keys[3], (BLOCKS,), 0, 6)
        length = 1 + first_draw * second_draw // 8
        anchor = jax.random.randint(keys[4], (), 0, BLOCKS)
        position = jnp.arange(BLOCKS, dtype=jnp.int32)
        length = jnp.where((position - anchor) % BLOCKS < LIST, LIST, length)
        length = jnp.minimum(length, LIST)
        column = jnp.arange(LIST, dtype=jnp.int32)
        entries = blocks_in_order[(position[:, None] + column[None, :]) % BLOCKS]
        entries = jnp.where(column[None, :] < length[:, None], entries, -1)
        return jnp.zeros((BLOCKS, LIST), jnp.int32).at[placed].set(entries.astype(jnp.int32))
    group_keys = jax.vmap(lambda number: jax.random.fold_in(base_key, number))(jnp.arange(GROUPS))
    tables = jax.vmap(one_group)(group_keys)
    return jnp.transpose(tables, (1, 0, 2)).astype(jnp.int32)


def draw_lists(key, part):
    return list_table(key)


def draw_labels(key, part):
    table = list_table(key)
    key = jax.random.fold_in(key, 11)
    keys = jax.random.split(key, 2)
    length = jnp.sum((table >= 0).astype(jnp.int32), axis=2)
    choose = jax.random.randint(keys[0], (BLOCKS, GROUPS, ROW_DEV), 0, 720720) % length[:, :, None]
    picked = jnp.take_along_axis(table, choose, axis=2)
    within = jax.random.randint(keys[1], (BLOCKS, GROUPS, ROW_DEV), 0, BLK)
    return (picked * BLK + within).astype(jnp.int32)


def draw_class_emb(key, part):
    key = jax.random.fold_in(key, 7)
    keys = jax.random.split(key, 3)
    big_scale = 60.0 / R ** 0.5
    near_scale = 2.0 / R ** 0.5
    phase = jnp.arange(CLASSES, dtype=jnp.int32)[:, None] % BLK
    big = jax.random.truncated_normal(keys[1], -4.0, 4.0, (CLASSES, R), jnp.float32)
    noise = jax.random.truncated_normal(keys[2], -4.0, 4.0, (CLASSES, R), jnp.float32)
    base = jax.random.truncated_normal(keys[0], -4.0, 4.0, (CLASSES, R), jnp.float32) * 0.265
    big = big * big_scale
    twin = jnp.roll(big, 1, axis=0) + near_scale * noise
    values = jnp.where(phase == 0, big, jnp.where(phase == 1, twin, base))
    return jnp.clip(values, -63.0, 63.0).astype(jnp.bfloat16)


def raised(values, rng, source, target, shards_of, factor):
    owner, partner = [(jnp.arange(values.shape[dim]) // (values.shape[dim] // shards_of)).reshape([-1 if axis == dim else 1 for axis in range(values.ndim)]) for dim in (source, target)]
    chosen = jax.random.permutation(rng, shards_of)[partner]
    strong = (owner == chosen) | (owner == (partner + shards_of // 2) % shards_of)
    return jnp.where(strong, factor * values, values)


def shard_levels(rng, dims, cuts, least, high):
    factor_of, own = 1.0, jax.random.fold_in(rng, 6)
    for dim, parts in cuts:
        draws = jnp.exp(jax.random.uniform(jax.random.fold_in(own, dim), (parts,), jnp.float32, least / len(cuts), high / len(cuts)))
        factor_of = factor_of * jnp.repeat(draws, dims[dim] // parts).reshape([-1 if axis == dim else 1 for axis in range(len(dims))])
    return factor_of


def gaussian(rng, extent, deviation, reach, cuts=(), held_as=jnp.bfloat16):
    factor_of = shard_levels(rng, extent, cuts, -0.22, 0.18) if cuts else 1.0
    values = jax.random.normal(rng, extent, jnp.float32) * deviation * factor_of
    return jnp.minimum(jnp.maximum(values, -reach), reach).astype(held_as)


def heavy_noise(key, extent, deviation, bound, cuts, heavy, kind=jnp.bfloat16):
    result = deviation * jax.random.normal(key, extent, jnp.float32)
    if cuts:
        result = result * shard_levels(key, extent, cuts, -0.22, 0.18)
    return jnp.clip(raised(result, jax.random.fold_in(key, 3), *heavy), -bound, bound).astype(kind)


def setup_inputs(seed: int = 0) -> dict:
    key_of = jax.random.split(jax.random.key(seed), 6)
    features = heavy_noise(key_of[0], (ROWS, D), 1.0, 24.0, ((0, 512),), (0, 1, 512, 6.0))
    proj = gaussian(key_of[1], (D, R), D ** -0.5, 0.09375)
    class_emb = draw_class_emb(jax.random.fold_in(key_of[5], 71), 0)
    lists = draw_lists(jax.random.fold_in(key_of[5], 71), 0)
    labels = draw_labels(jax.random.fold_in(key_of[5], 71), 0)
    return dict(features=features, proj=proj, class_emb=class_emb, lists=lists, labels=labels)


NEG = -1e30


def block_scores(rows_in, factors):
    return lax.dot_general(rows_in, factors, (((1,), (1,)), ((), ())), preferred_element_type=jnp.float32)


def reference(features, proj, class_emb, lists, labels):
    hidden = jnp.dot(features, proj, preferred_element_type=jnp.float32).astype(jnp.bfloat16)
    hidden = hidden.reshape(BLOCKS, GROUPS, ROW_DEV, R)
    factors = class_emb.reshape(BLOCKS, BLK, R)
    block_ids = jnp.arange(BLOCKS, dtype=jnp.int32)
    listed = jnp.any(lists[:, :, :, None] == block_ids[None, None, None, :], axis=2)
    list_rank = (jnp.cumsum(listed.astype(jnp.int32), axis=0) - 1).astype(jnp.int32)
    live_counts = jnp.sum(listed.astype(jnp.int32), axis=0).astype(jnp.int32)
    slot_ids = jnp.arange(LIST, dtype=jnp.int32)
    chosen = (list_rank[None] == slot_ids[:, None, None, None]) & listed[None]
    source_of = jnp.sum(jnp.where(chosen, block_ids[None, :, None, None], 0), axis=1).astype(jnp.int32)
    class_ids = jnp.arange(BLK, dtype=jnp.int32)

    def stats_pair(block, group, slot_index, carry):
        peak_all, mass_all, label_all = carry
        source = source_of[slot_index, group, block]
        scores = block_scores(hidden[source, group], factors[block])
        peak = jnp.max(scores, axis=1)
        mass = jnp.sum(jnp.exp(scores - peak[:, None]), axis=1)
        label_local = labels[source, group] - block * BLK
        inside = (label_local >= 0) & (label_local < BLK)
        label_score = jnp.take_along_axis(scores, jnp.clip(label_local, 0, BLK - 1)[:, None], axis=1)[:, 0]
        label_score = jnp.where(inside, label_score, NEG)
        old_peak = peak_all[source, group]
        new_peak = jnp.maximum(old_peak, peak)
        new_mass = mass_all[source, group] * jnp.exp(old_peak - new_peak) + mass * jnp.exp(peak - new_peak)
        peak_all = peak_all.at[source, group].set(new_peak)
        mass_all = mass_all.at[source, group].set(new_mass)
        label_all = label_all.at[source, group].set(jnp.maximum(label_all[source, group], label_score))
        return peak_all, mass_all, label_all

    def stats_block(block, carry):
        def stats_group(group, inner):
            return lax.fori_loop(jnp.int32(0), live_counts[group, block], lambda slot_index, state: stats_pair(block, group, slot_index, state), inner)
        return lax.fori_loop(0, GROUPS, stats_group, carry)

    start = (jnp.full((BLOCKS, GROUPS, ROW_DEV), NEG, jnp.float32), jnp.zeros((BLOCKS, GROUPS, ROW_DEV), jnp.float32), jnp.full((BLOCKS, GROUPS, ROW_DEV), NEG, jnp.float32))
    peak_all, mass_all, label_all = lax.fori_loop(0, BLOCKS, stats_block, start)
    log_norm = peak_all + jnp.log(mass_all)
    loss = (log_norm - label_all).reshape(ROWS)

    def grad_pair(block, group, slot_index, carry):
        back_sum, block_part = carry
        source = source_of[slot_index, group, block]
        rows_in = hidden[source, group]
        scores = block_scores(rows_in, factors[block])
        probs = jnp.exp(scores - log_norm[source, group][:, None])
        label_local = labels[source, group] - block * BLK
        target = (class_ids[None, :] == label_local[:, None]).astype(jnp.float32)
        weights = (probs - target).astype(jnp.bfloat16)
        block_part = block_part + lax.dot_general(weights, rows_in, (((0,), (0,)), ((), ())), preferred_element_type=jnp.float32)
        back_rows = lax.optimization_barrier(jnp.dot(weights, factors[block], preferred_element_type=jnp.float32).astype(jnp.bfloat16))
        back_sum = back_sum.at[source, group].add(back_rows.astype(jnp.float32))
        return back_sum, block_part

    def grad_block(block, carry):
        back_sum, class_grad = carry

        def grad_group(group, inner):
            back_inner, block_total = inner
            zero_part = jnp.zeros((BLK, R), jnp.float32)
            back_inner, block_part = lax.fori_loop(jnp.int32(0), live_counts[group, block], lambda slot_index, state: grad_pair(block, group, slot_index, state), (back_inner, zero_part))
            rounded = lax.optimization_barrier(block_part.astype(jnp.bfloat16))
            return back_inner, block_total + rounded.astype(jnp.float32)

        back_sum, block_total = lax.fori_loop(0, GROUPS, grad_group, (back_sum, jnp.zeros((BLK, R), jnp.float32)))
        class_grad = lax.dynamic_update_index_in_dim(class_grad, block_total, block, 0)
        return back_sum, class_grad

    back_start = jnp.zeros((BLOCKS, GROUPS, ROW_DEV, R), jnp.float32)
    grad_start = jnp.zeros((BLOCKS, BLK, R), jnp.float32)
    back_sum, class_grad = lax.fori_loop(0, BLOCKS, grad_block, (back_start, grad_start))
    row_grad = back_sum.astype(jnp.bfloat16).reshape(BLOCKS * GROUPS, ROW_DEV, R)
    row_feats = features.reshape(BLOCKS * GROUPS, ROW_DEV, D)

    def add_block(block_index, total):
        return total + lax.dot_general(row_feats[block_index], row_grad[block_index], (((0,), (0,)), ((), ())), preferred_element_type=jnp.float32)

    proj_grad = lax.fori_loop(0, BLOCKS * GROUPS, add_block, jnp.zeros((D, R), jnp.float32))
    return loss, class_grad.reshape(CLASSES, R), proj_grad
```

```python
import jax
import jax.numpy as jnp
from jax import lax
from jax.experimental import pallas as pl
from jax.experimental.pallas import tpu as pltpu
from jax.sharding import PartitionSpec as P

LIST = 6
NX, NY, NK = 4, 8, 2
TILE = 1024
NEG = -1e30
F32 = jnp.float32
BF16 = jnp.bfloat16
GROUP_Y = [[x * 16 + y * 2 + k for y in range(NY)] for x in range(NX) for k in range(NK)]
GROUP_X = [[x * 16 + y * 2 + k for x in range(NX)] for y in range(NY) for k in range(NK)]
SWAP_K = [(c, c ^ 1) for c in range(NX * NY * NK)]


def exchange(value, groups):
    return lax.all_to_all(value, "cls", 0, 0, axis_index_groups=groups, tiled=True)


def spread(value, count):
    return jnp.broadcast_to(value[None], (count,) + value.shape)


def gather_cls(block):
    along_y = exchange(spread(block, NY), GROUP_Y)
    own = exchange(spread(along_y, NX), GROUP_X).reshape((NX * NY,) + block.shape)
    return own, lax.ppermute(own, "cls", SWAP_K)


def scatter_cls(outbox):
    swapped = lax.ppermute(outbox[1], "cls", SWAP_K)
    total = (outbox[0].astype(F32) + swapped.astype(F32)).astype(BF16)
    total = jnp.sum(exchange(total, GROUP_X), axis=0, dtype=F32).astype(BF16)
    return jnp.sum(exchange(total, GROUP_Y), axis=0, dtype=F32).astype(BF16)


def scores_of(factors, rows):
    return lax.dot_general(factors, rows, (((1,), (1,)), ((), ())), preferred_element_type=F32)


def stats_kernel(slots_ref, own_ref, other_ref, label_ref, emb_ref, rows_ref, stat_ref, peak_ref, mass_ref, score_ref):
    step = pl.program_id(0)
    width = rows_ref.shape[0] // LIST

    @pl.when(step == 0)
    def _():
        for slot in range(LIST):
            place = slots_ref[slot]
            near = own_ref[lax.rem(place, NX * NY)]
            far = other_ref[lax.rem(place, NX * NY)]
            rows_ref[slot * width:(slot + 1) * width, :] = jnp.where(place < NX * NY, near, far)
        peak_ref[...] = jnp.full(peak_ref.shape, NEG, F32)
        mass_ref[...] = jnp.zeros(mass_ref.shape, F32)
        score_ref[...] = jnp.zeros(score_ref.shape, F32)

    factors = emb_ref[...]
    tile = factors.shape[0]
    class_ids = lax.broadcasted_iota(jnp.int32, (tile // 8, 8, 2 * width), 0) * 8 + lax.broadcasted_iota(jnp.int32, (tile // 8, 8, 2 * width), 1)
    for pair in range(LIST // 2):
        cut = slice(pair * 2 * width, (pair + 1) * 2 * width)
        scores = scores_of(factors, rows_ref[cut, :]).reshape(tile // 8, 8, 2 * width)
        local_label = label_ref[0:1, cut] - step * tile
        hit = class_ids == local_label[None]
        score_ref[:, cut] += jnp.sum(jnp.where(hit, scores, 0.0), axis=0)
        old = peak_ref[:, cut]
        new = jnp.maximum(old, jnp.max(scores, axis=0))
        mass_ref[:, cut] = mass_ref[:, cut] * jnp.exp(old - new) + jnp.sum(jnp.exp(scores - new[None]), axis=0)
        peak_ref[:, cut] = new

    @pl.when(step == pl.num_programs(0) - 1)
    def _():
        peak = jnp.max(peak_ref[...], axis=0, keepdims=True)
        mass = jnp.sum(mass_ref[...] * jnp.exp(peak_ref[...] - peak), axis=0, keepdims=True)
        norm = peak + jnp.log(mass)
        score = jnp.sum(score_ref[...], axis=0, keepdims=True)
        stat_ref[...] = jnp.zeros(stat_ref.shape, F32)
        for slot in range(LIST):
            stat_ref[slot:slot + 1, :] = norm[:, slot * width:(slot + 1) * width]
            stat_ref[8 + slot:9 + slot, :] = score[:, slot * width:(slot + 1) * width]


def grads_kernel(slots_ref, live_ref, query_ref, stat_ref, label_ref, rows_ref, emb_ref, part_ref, back_ref, loss_ref, norm_ref, total_ref):
    step = pl.program_id(0)
    width = rows_ref.shape[0] // LIST

    def combined(which):
        norms, label_score = [], jnp.zeros((1, width), F32)
        for entry in range(LIST):
            place = query_ref[which * LIST + entry]
            base = jnp.maximum(place, 0)
            norm = stat_ref[pl.ds(base, 1), :]
            score = stat_ref[pl.ds(base + 8, 1), :]
            norms.append(jnp.where(place >= 0, norm, NEG))
            label_score = label_score + jnp.where(place >= 0, score, 0.0)
        peak = norms[0]
        for norm in norms[1:]:
            peak = jnp.maximum(peak, norm)
        mass = jnp.zeros((1, width), F32)
        for norm in norms:
            mass = mass + jnp.exp(norm - peak)
        return peak + jnp.log(mass), label_score

    @pl.when(step == 0)
    def _():
        for slot in range(LIST):
            norm, _ = combined(slot)
            norm_ref[0:1, slot * width:(slot + 1) * width] = jnp.where(slot < live_ref[0], norm, -NEG)
        norm, label_score = combined(LIST)
        loss_ref[...] = norm - label_score
        total_ref[...] = jnp.zeros(total_ref.shape, F32)
        back_ref[...] = jnp.zeros(back_ref.shape, BF16)

    factors = emb_ref[...]
    tile = factors.shape[0]
    rows = rows_ref[...]
    scores = scores_of(factors, rows)
    probs = jnp.exp(scores - norm_ref[0:1, :])
    class_ids = lax.broadcasted_iota(jnp.int32, scores.shape, 0)
    hit = class_ids == label_ref[0:1, :] - step * tile
    weights = jnp.where(hit, probs - 1.0, probs).astype(BF16)
    part_ref[...] = jnp.dot(weights, rows, preferred_element_type=F32).astype(BF16)
    total_ref[...] += lax.dot_general(factors, weights, (((0,), (0,)), ((), ())), preferred_element_type=F32)

    @pl.when(step == pl.num_programs(0) - 1)
    def _():
        for slot in range(LIST):
            @pl.when(slot < live_ref[0])
            def _():
                back_ref[slots_ref[slot]] = total_ref[:, slot * width:(slot + 1) * width].T.astype(BF16)


def column_order(features, parts):
    rows, depth = features.shape
    span = parts * 128
    source = lax.broadcasted_iota(jnp.int32, (span, span), 0)
    target = lax.broadcasted_iota(jnp.int32, (span, span), 1)
    group, rest = target // 128, target % 128
    wanted = (rest // 8) * (8 * parts) + group * 8 + rest % 8
    permutation = (source == wanted).astype(BF16)
    chunks = features.reshape(rows * (depth // span), span)
    moved = jnp.dot(chunks, permutation, preferred_element_type=F32).astype(BF16)
    moved = moved.reshape(rows, depth // span, parts, 128)
    return jnp.transpose(moved, (2, 0, 1, 3)).reshape(parts, rows, depth // parts)


def local(features, proj, class_emb, lists, labels):
    blocks = lax.axis_size("cls")
    groups = lax.axis_size("dp")
    own_block = lax.axis_index("cls")
    width = features.shape[0]
    block_width, rank_width = class_emb.shape
    hidden = jnp.dot(features, proj, preferred_element_type=F32).astype(BF16)
    near, far = gather_cls(hidden)

    table = lists[:, 0, :]
    group_labels = labels[:, 0, :]
    block_ids = jnp.arange(blocks, dtype=jnp.int32)
    places = ((block_ids ^ own_block) & 1) * (NX * NY) + block_ids // 2
    listed_by = jnp.any(table == own_block, axis=1)
    list_rank = jnp.cumsum(listed_by.astype(jnp.int32)) - 1
    live = jnp.sum(listed_by.astype(jnp.int32))
    slot_ids = jnp.arange(LIST, dtype=jnp.int32)
    chosen = (list_rank[None, :] == slot_ids[:, None]) & listed_by[None, :]
    slot_places = jnp.sum(jnp.where(chosen, places[None, :], 0), axis=1)
    same = (table[:, :, None, None] == table[None, None]) & (block_ids[None, None, :, None] < block_ids[:, None, None, None])
    entry_rank = jnp.sum(same.astype(jnp.int32), axis=(2, 3))
    entry_place = (((table ^ own_block) & 1) * (NX * NY) + table // 2) * 16 + entry_rank
    entry_place = jnp.where(table >= 0, entry_place, -1)
    asked = jnp.concatenate([chosen, (block_ids == own_block)[None]], axis=0)
    queries = jnp.sum(jnp.where(asked[:, :, None], entry_place[None], 0), axis=1).reshape(-1)
    slot_labels = jnp.sum(jnp.where(chosen[:, :, None], group_labels[None], 0), axis=1)
    slot_labels = jnp.where(slot_ids[:, None] < live, slot_labels - own_block * block_width, -1)
    slot_labels = spread(slot_labels.reshape(-1), 8)

    steps = block_width // TILE
    all_rows = LIST * width
    smem = pl.BlockSpec(memory_space=pltpu.SMEM)
    whole = pl.BlockSpec(memory_space=pltpu.VMEM)
    tiled = pl.BlockSpec((TILE, rank_width), lambda i: (i, 0))
    fixed = lambda shape: pl.BlockSpec(shape, lambda i: (0,) * len(shape))
    params = pltpu.CompilerParams(vmem_limit_bytes=48 * 1024 * 1024)
    rows, stats = pl.pallas_call(
        stats_kernel,
        grid=(steps,),
        in_specs=[smem, whole, whole, whole, tiled],
        out_specs=[fixed((all_rows, rank_width)), fixed((16, width))],
        out_shape=[jax.ShapeDtypeStruct((all_rows, rank_width), BF16), jax.ShapeDtypeStruct((16, width), F32)],
        scratch_shapes=[pltpu.VMEM((8, all_rows), F32)] * 3,
        compiler_params=params,
    )(slot_places, near, far, slot_labels, class_emb)

    stats_near, stats_far = gather_cls(stats)
    all_stats = jnp.concatenate([stats_near, stats_far], axis=0).reshape(-1, width)
    class_part, outbox, loss = pl.pallas_call(
        grads_kernel,
        grid=(steps,),
        in_specs=[smem, smem, smem, whole, whole, whole, tiled],
        out_specs=[tiled, fixed((blocks, width, rank_width)), fixed((1, width))],
        out_shape=[
            jax.ShapeDtypeStruct((block_width, rank_width), BF16),
            jax.ShapeDtypeStruct((blocks, width, rank_width), BF16),
            jax.ShapeDtypeStruct((1, width), F32),
        ],
        scratch_shapes=[pltpu.VMEM((8, all_rows), F32), pltpu.VMEM((rank_width, all_rows), F32)],
        compiler_params=params,
    )(slot_places, live.reshape(1), queries, all_stats, slot_labels, rows, class_emb)

    class_grad = lax.psum_scatter(class_part, "dp", scatter_dimension=0, tiled=True).astype(F32)
    columns = lax.all_to_all(column_order(features, groups), "dp", 0, 0, tiled=True)
    columns = columns.reshape(groups * width, -1)
    row_grad = scatter_cls(outbox.reshape(NK, NX, NY, width, rank_width))
    row_grads = lax.all_to_all(spread(row_grad, groups), "dp", 0, 0, tiled=True).reshape(groups * width, rank_width)
    proj_part = lax.dot_general(columns, row_grads, (((0,), (0,)), ((), ())), preferred_element_type=F32)
    share = proj_part.shape[0] // blocks
    arrived = lax.all_to_all(proj_part.reshape(blocks, share, rank_width), "cls", 0, 0, tiled=True)
    proj_grad = jnp.sum(arrived, axis=0)
    return loss.reshape(-1), class_grad, proj_grad


def solution(mesh):
    in_specs = (
        P(("cls", "dp"), None),
        P(),
        P("cls", None),
        P(None, "dp", None),
        P(None, "dp", None),
    )
    out_specs = (P(("cls", "dp")), P(("cls", "dp"), None), P(("cls", "dp"), None))
    return jax.shard_map(local, mesh=mesh, in_specs=in_specs, out_specs=out_specs, check_vma=False)
```

```python
import jax
import jax.numpy as jnp
from jax import lax
from jax.experimental import pallas as pl
from jax.experimental.pallas import tpu as pltpu
from jax.sharding import PartitionSpec as P

LIST = 6
NX, NY, NK = 4, 8, 2
TILE = 1024
NEG = -1e30
F32 = jnp.float32
BF16 = jnp.bfloat16
GROUP_Y = [[x * 16 + y * 2 + k for y in range(NY)] for x in range(NX) for k in range(NK)]
GROUP_X = [[x * 16 + y * 2 + k for x in range(NX)] for y in range(NY) for k in range(NK)]
SWAP_K = [(c, c ^ 1) for c in range(NX * NY * NK)]


def exchange(value, groups):
    return lax.all_to_all(value, "cls", 0, 0, axis_index_groups=groups, tiled=True)


def spread(value, count):
    return jnp.broadcast_to(value[None], (count,) + value.shape)


def gather_cls(block):
    return gather_xk(exchange(spread(block, NY), GROUP_Y), block.shape)


def gather_xk(along_y, shape):
    own = exchange(spread(along_y, NX), GROUP_X).reshape((NX * NY,) + shape)
    return own, lax.ppermute(own, "cls", SWAP_K)


def swap_bit(buffer, axis, bit):
    arrived = lax.ppermute(lax.index_in_dim(buffer, 1, axis, keepdims=False), "dp", [(z, z ^ bit) for z in range(8)])
    return jnp.stack([lax.index_in_dim(buffer, 0, axis, keepdims=False), arrived], axis=axis)


def scatter_cls(kept, swapped):
    total = (kept.astype(F32) + swapped.astype(F32)).astype(BF16)
    total = jnp.sum(exchange(total, GROUP_X), axis=0, dtype=F32).astype(BF16)
    return jnp.sum(exchange(total, GROUP_Y), axis=0, dtype=F32).astype(BF16)


def scores_of(factors, rows):
    return lax.dot_general(factors, rows, (((1,), (1,)), ((), ())), preferred_element_type=F32)


def stats_kernel(slots_ref, own_ref, other_ref, target_ref, emb_ref, rows_ref, stat_ref, peak_ref, mass_ref):
    step = pl.program_id(0)
    width = rows_ref.shape[0] // LIST

    @pl.when(step == 0)
    def _():
        for slot in range(LIST):
            place = slots_ref[slot]
            near = own_ref[lax.rem(place, NX * NY)]
            far = other_ref[lax.rem(place, NX * NY)]
            rows_ref[slot * width:(slot + 1) * width, :] = jnp.where(place < NX * NY, near, far)
        peak_ref[...] = jnp.full(peak_ref.shape, NEG, F32)
        mass_ref[...] = jnp.zeros(mass_ref.shape, F32)

    factors = emb_ref[...]
    tile = factors.shape[0]
    for pair in range(LIST // 2):
        cut = slice(pair * 2 * width, (pair + 1) * 2 * width)
        scores = scores_of(factors, rows_ref[cut, :]).reshape(tile // 8, 8, 2 * width)
        old = peak_ref[:, cut]
        new = jnp.maximum(old, jnp.max(scores, axis=0))
        mass_ref[:, cut] = mass_ref[:, cut] * jnp.exp(old - new) + jnp.sum(jnp.exp(scores - new[None]), axis=0)
        peak_ref[:, cut] = new

    @pl.when(step == pl.num_programs(0) - 1)
    def _():
        peak = jnp.max(peak_ref[...], axis=0, keepdims=True)
        mass = jnp.sum(mass_ref[...] * jnp.exp(peak_ref[...] - peak), axis=0, keepdims=True)
        norm = peak + jnp.log(mass)
        products = rows_ref[...].astype(F32) * target_ref[...].astype(F32)
        ones = jnp.ones((8, products.shape[1]), F32)
        score = lax.dot_general(ones, products, (((1,), (1,)), ((), ())), precision=lax.Precision.HIGHEST, preferred_element_type=F32)
        stat_ref[...] = jnp.zeros(stat_ref.shape, F32)
        for slot in range(LIST):
            stat_ref[slot:slot + 1, :] = norm[:, slot * width:(slot + 1) * width]
            stat_ref[8 + slot:9 + slot, :] = score[0:1, slot * width:(slot + 1) * width]


def weights_of(step, factors, rows, norm_ref, label_ref):
    scores = scores_of(factors, rows)
    probs = jnp.exp(scores - norm_ref[0:1, :])
    class_ids = lax.broadcasted_iota(jnp.int32, scores.shape, 0)
    hit = class_ids == label_ref[0:1, :] - step * factors.shape[0]
    return jnp.where(hit, probs - 1.0, probs).astype(BF16)


def part_kernel(norm_ref, label_ref, rows_ref, emb_ref, part_ref):
    rows = rows_ref[...]
    weights = weights_of(pl.program_id(0), emb_ref[...], rows, norm_ref, label_ref)
    part_ref[...] = jnp.dot(weights, rows, preferred_element_type=F32).astype(BF16)


def back_kernel(slots_ref, live_ref, query_ref, stat_ref, label_ref, rows_ref, emb_ref, back_ref, loss_ref, norm_ref, total_ref):
    step = pl.program_id(0)
    width = rows_ref.shape[0] // LIST

    def combined(which):
        norms, label_score = [], jnp.zeros((1, width), F32)
        for entry in range(LIST):
            place = query_ref[which * LIST + entry]
            base = jnp.maximum(place, 0)
            norm = stat_ref[pl.ds(base, 1), :]
            score = stat_ref[pl.ds(base + 8, 1), :]
            norms.append(jnp.where(place >= 0, norm, NEG))
            label_score = label_score + jnp.where(place >= 0, score, 0.0)
        peak = norms[0]
        for norm in norms[1:]:
            peak = jnp.maximum(peak, norm)
        mass = jnp.zeros((1, width), F32)
        for norm in norms:
            mass = mass + jnp.exp(norm - peak)
        return peak + jnp.log(mass), label_score

    @pl.when(step == 0)
    def _():
        for slot in range(LIST):
            norm, _ = combined(slot)
            norm_ref[0:1, slot * width:(slot + 1) * width] = jnp.where(slot < live_ref[0], norm, -NEG)
        norm, label_score = combined(LIST)
        loss_ref[...] = norm - label_score
        total_ref[...] = jnp.zeros(total_ref.shape, F32)
        back_ref[...] = jnp.zeros(back_ref.shape, BF16)

    factors = emb_ref[...]
    weights = weights_of(step, factors, rows_ref[...], norm_ref, label_ref)
    total_ref[...] += lax.dot_general(factors, weights, (((0,), (0,)), ((), ())), preferred_element_type=F32)

    @pl.when(step == pl.num_programs(0) - 1)
    def _():
        for slot in range(LIST):
            @pl.when(slot < live_ref[0])
            def _():
                back_ref[slots_ref[slot]] = total_ref[:, slot * width:(slot + 1) * width].T.astype(BF16)


def column_order(features, parts, own):
    rows, depth = features.shape
    span = parts * 128
    source = lax.broadcasted_iota(jnp.int32, (span, span), 0)
    target = lax.broadcasted_iota(jnp.int32, (span, span), 1)
    group, rest = (target // 128) ^ own, target % 128
    wanted = (rest // 8) * (8 * parts) + group * 8 + rest % 8
    permutation = (source == wanted).astype(BF16)
    chunks = features.reshape(rows * (depth // span), span)
    moved = jnp.dot(chunks, permutation, preferred_element_type=F32).astype(BF16)
    moved = moved.reshape(rows, depth // span, parts, 128)
    return jnp.transpose(moved, (2, 0, 1, 3)).reshape(parts, rows, depth // parts)


def local(features, proj, class_emb, lists, labels):
    blocks = lax.axis_size("cls")
    groups = lax.axis_size("dp")
    own_block = lax.axis_index("cls")
    width = features.shape[0]
    block_width, rank_width = class_emb.shape
    hidden = jnp.dot(features, proj, preferred_element_type=F32).astype(BF16)
    own_group = lax.axis_index("dp")
    along_y = exchange(spread(hidden, NY), GROUP_Y)
    late_features, along_y = lax.optimization_barrier((features, along_y))
    columns = column_order(late_features, groups, own_group).reshape(2, 2, 2, width, -1)
    near, far = gather_xk(along_y, hidden.shape)
    columns, far = lax.optimization_barrier((columns, far))
    columns = swap_bit(columns, 0, 4)

    table = lists[:, 0, :]
    group_labels = labels[:, 0, :]
    block_ids = jnp.arange(blocks, dtype=jnp.int32)
    places = ((block_ids ^ own_block) & 1) * (NX * NY) + block_ids // 2
    listed_by = jnp.any(table == own_block, axis=1)
    list_rank = jnp.cumsum(listed_by.astype(jnp.int32)) - 1
    live = jnp.sum(listed_by.astype(jnp.int32))
    slot_ids = jnp.arange(LIST, dtype=jnp.int32)
    chosen = (list_rank[None, :] == slot_ids[:, None]) & listed_by[None, :]
    slot_places = jnp.sum(jnp.where(chosen, places[None, :], 0), axis=1)
    same = (table[:, :, None, None] == table[None, None]) & (block_ids[None, None, :, None] < block_ids[:, None, None, None])
    entry_rank = jnp.sum(same.astype(jnp.int32), axis=(2, 3))
    entry_place = (((table ^ own_block) & 1) * (NX * NY) + table // 2) * 16 + entry_rank
    entry_place = jnp.where(table >= 0, entry_place, -1)
    asked = jnp.concatenate([chosen, (block_ids == own_block)[None]], axis=0)
    queries = jnp.sum(jnp.where(asked[:, :, None], entry_place[None], 0), axis=1).reshape(-1)
    slot_labels = jnp.sum(jnp.where(chosen[:, :, None], group_labels[None], 0), axis=1)
    slot_labels = jnp.where(slot_ids[:, None] < live, slot_labels - own_block * block_width, -1)
    slot_labels = slot_labels.reshape(-1)
    inside = (slot_labels >= 0) & (slot_labels < block_width)
    targets = jnp.take(class_emb, jnp.clip(slot_labels, 0, block_width - 1), axis=0, mode="clip")
    targets = jnp.where(inside[:, None], targets, jnp.zeros((), BF16))
    slot_labels = spread(slot_labels, 8)

    steps = block_width // TILE
    all_rows = LIST * width
    smem = pl.BlockSpec(memory_space=pltpu.SMEM)
    whole = pl.BlockSpec(memory_space=pltpu.VMEM)
    tiled = pl.BlockSpec((TILE, rank_width), lambda i: (i, 0))
    fixed = lambda shape: pl.BlockSpec(shape, lambda i: (0,) * len(shape))
    params = pltpu.CompilerParams(vmem_limit_bytes=48 * 1024 * 1024)
    rows, stats = pl.pallas_call(
        stats_kernel,
        grid=(steps,),
        in_specs=[smem, whole, whole, whole, tiled],
        out_specs=[fixed((all_rows, rank_width)), fixed((16, width))],
        out_shape=[jax.ShapeDtypeStruct((all_rows, rank_width), BF16), jax.ShapeDtypeStruct((16, width), F32)],
        scratch_shapes=[pltpu.VMEM((8, all_rows), F32)] * 2,
        compiler_params=params,
    )(slot_places, near, far, targets, class_emb)

    columns, stats = lax.optimization_barrier((columns, stats))
    columns = swap_bit(columns, 1, 2)
    stats_near, stats_far = gather_cls(stats)
    columns, stats_far = lax.optimization_barrier((columns, stats_far))
    all_stats = jnp.concatenate([stats_near, stats_far], axis=0).reshape(-1, width)
    outbox, loss, norms = pl.pallas_call(
        back_kernel,
        grid=(steps,),
        in_specs=[smem, smem, smem, whole, whole, whole, tiled],
        out_specs=[fixed((blocks, width, rank_width)), fixed((1, width)), fixed((8, all_rows))],
        out_shape=[
            jax.ShapeDtypeStruct((blocks, width, rank_width), BF16),
            jax.ShapeDtypeStruct((1, width), F32),
            jax.ShapeDtypeStruct((8, all_rows), F32),
        ],
        scratch_shapes=[pltpu.VMEM((rank_width, all_rows), F32)],
        compiler_params=params,
    )(slot_places, live.reshape(1), queries, all_stats, slot_labels, rows, class_emb)

    outbox = outbox.reshape(NK, NX, NY, width, rank_width)
    swapped, columns, rows = lax.optimization_barrier((lax.ppermute(outbox[1], "cls", SWAP_K), columns, rows))
    columns = swap_bit(columns, 2, 1)
    class_part = pl.pallas_call(
        part_kernel,
        grid=(steps,),
        in_specs=[whole, whole, whole, tiled],
        out_specs=tiled,
        out_shape=jax.ShapeDtypeStruct((block_width, rank_width), BF16),
        compiler_params=params,
    )(norms, slot_labels, rows, class_emb)
    class_grad = lax.psum_scatter(class_part, "dp", scatter_dimension=0, tiled=True).astype(F32)
    row_grad = scatter_cls(outbox[0], swapped)
    columns, row_grad = lax.optimization_barrier((columns, row_grad))
    columns = columns.reshape(groups, width, -1)
    columns = jnp.take(columns, jnp.arange(groups, dtype=jnp.int32) ^ own_group, axis=0, mode="clip").reshape(groups * width, -1)
    row_grads = lax.all_to_all(spread(row_grad, groups), "dp", 0, 0, tiled=True).reshape(groups * width, rank_width)
    proj_part = lax.dot_general(columns, row_grads, (((0,), (0,)), ((), ())), preferred_element_type=F32)
    share = proj_part.shape[0] // blocks
    arrived = lax.all_to_all(proj_part.reshape(blocks, share, rank_width), "cls", 0, 0, tiled=True)
    proj_grad = jnp.sum(arrived, axis=0)
    return loss.reshape(-1), class_grad, proj_grad


def solution(mesh):
    in_specs = (
        P(("cls", "dp"), None),
        P(),
        P("cls", None),
        P(None, "dp", None),
        P(None, "dp", None),
    )
    out_specs = (P(("cls", "dp")), P(("cls", "dp"), None), P(("cls", "dp"), None))
    return jax.shard_map(local, mesh=mesh, in_specs=in_specs, out_specs=out_specs, check_vma=False)
```

```python
import jax
import jax.numpy as jnp
from jax import lax
from jax.experimental import pallas as pl
from jax.experimental.pallas import tpu as pltpu
from jax.sharding import PartitionSpec as P

LIST = 6
NX, NY, NK = 4, 8, 2
TILE = 1024
NEG = -1e30
F32 = jnp.float32
BF16 = jnp.bfloat16
GROUP_Y = [[x * 16 + y * 2 + k for y in range(NY)] for x in range(NX) for k in range(NK)]
GROUP_X = [[x * 16 + y * 2 + k for x in range(NX)] for y in range(NY) for k in range(NK)]
SWAP_K = [(c, c ^ 1) for c in range(NX * NY * NK)]


def exchange(value, groups):
    return lax.all_to_all(value, "cls", 0, 0, axis_index_groups=groups, tiled=True)


def spread(value, count):
    return jnp.broadcast_to(value[None], (count,) + value.shape)


def gather_cls(block):
    along_y = exchange(spread(block, NY), GROUP_Y)
    own = exchange(spread(along_y, NX), GROUP_X).reshape((NX * NY,) + block.shape)
    return own, lax.ppermute(own, "cls", SWAP_K)


def scatter_cls(outbox):
    swapped = lax.ppermute(outbox[1], "cls", SWAP_K)
    total = (outbox[0].astype(F32) + swapped.astype(F32)).astype(BF16)
    total = jnp.sum(exchange(total, GROUP_X), axis=0, dtype=F32).astype(BF16)
    return jnp.sum(exchange(total, GROUP_Y), axis=0, dtype=F32).astype(BF16)


def scores_of(factors, rows):
    return lax.dot_general(factors, rows, (((1,), (1,)), ((), ())), preferred_element_type=F32)


def stats_kernel(slots_ref, own_ref, other_ref, target_ref, emb_ref, rows_ref, stat_ref, peak_ref, mass_ref):
    step = pl.program_id(0)
    width = rows_ref.shape[0] // LIST

    @pl.when(step == 0)
    def _():
        for slot in range(LIST):
            place = slots_ref[slot]
            near = own_ref[lax.rem(place, NX * NY)]
            far = other_ref[lax.rem(place, NX * NY)]
            rows_ref[slot * width:(slot + 1) * width, :] = jnp.where(place < NX * NY, near, far)
        peak_ref[...] = jnp.full(peak_ref.shape, NEG, F32)
        mass_ref[...] = jnp.zeros(mass_ref.shape, F32)

    factors = emb_ref[...]
    tile = factors.shape[0]
    for pair in range(LIST // 2):
        cut = slice(pair * 2 * width, (pair + 1) * 2 * width)
        scores = scores_of(factors, rows_ref[cut, :]).reshape(tile // 8, 8, 2 * width)
        old = peak_ref[:, cut]
        new = jnp.maximum(old, jnp.max(scores, axis=0))
        mass_ref[:, cut] = mass_ref[:, cut] * jnp.exp(old - new) + jnp.sum(jnp.exp(scores - new[None]), axis=0)
        peak_ref[:, cut] = new

    @pl.when(step == pl.num_programs(0) - 1)
    def _():
        peak = jnp.max(peak_ref[...], axis=0, keepdims=True)
        mass = jnp.sum(mass_ref[...] * jnp.exp(peak_ref[...] - peak), axis=0, keepdims=True)
        norm = peak + jnp.log(mass)
        products = rows_ref[...].astype(F32) * target_ref[...].astype(F32)
        ones = jnp.ones((8, products.shape[1]), F32)
        score = lax.dot_general(ones, products, (((1,), (1,)), ((), ())), precision=lax.Precision.HIGHEST, preferred_element_type=F32)
        for slot in range(LIST):
            stat_ref[slot:slot + 1, :] = norm[:, slot * width:(slot + 1) * width]
            stat_ref[LIST + slot:LIST + 1 + slot, :] = score[0:1, slot * width:(slot + 1) * width]


def grads_kernel(slots_ref, live_ref, query_ref, stat_ref, label_ref, rows_ref, emb_ref, part_ref, back_ref, loss_ref, norm_ref, total_ref):
    step = pl.program_id(0)
    width = rows_ref.shape[0] // LIST

    def combined(which):
        norms, label_score = [], jnp.zeros((1, width), F32)
        for entry in range(LIST):
            place = query_ref[which * LIST + entry]
            base = jnp.maximum(place, 0)
            block, rank = base // (2 * LIST), lax.rem(base, 2 * LIST)
            norm = stat_ref[block, pl.ds(rank, 1), :]
            score = stat_ref[block, pl.ds(rank + LIST, 1), :]
            norms.append(jnp.where(place >= 0, norm, NEG))
            label_score = label_score + jnp.where(place >= 0, score, 0.0)
        peak = norms[0]
        for norm in norms[1:]:
            peak = jnp.maximum(peak, norm)
        mass = jnp.zeros((1, width), F32)
        for norm in norms:
            mass = mass + jnp.exp(norm - peak)
        return peak + jnp.log(mass), label_score

    @pl.when(step == 0)
    def _():
        for slot in range(LIST):
            norm, _ = combined(slot)
            norm_ref[0:1, slot * width:(slot + 1) * width] = jnp.where(slot < live_ref[0], norm, -NEG)
        norm, label_score = combined(LIST)
        loss_ref[...] = norm - label_score
        total_ref[...] = jnp.zeros(total_ref.shape, F32)
        back_ref[...] = jnp.zeros(back_ref.shape, BF16)

    factors = emb_ref[...]
    tile = factors.shape[0]
    rows = rows_ref[...]
    scores = scores_of(factors, rows)
    probs = jnp.exp(scores - norm_ref[0:1, :])
    class_ids = lax.broadcasted_iota(jnp.int32, scores.shape, 0)
    hit = class_ids == label_ref[0:1, :] - step * tile
    weights = jnp.where(hit, probs - 1.0, probs).astype(BF16)
    part_ref[...] = jnp.dot(weights, rows, preferred_element_type=F32).astype(BF16)
    total_ref[...] += lax.dot_general(factors, weights, (((0,), (0,)), ((), ())), preferred_element_type=F32)

    @pl.when(step == pl.num_programs(0) - 1)
    def _():
        for slot in range(LIST):
            @pl.when(slot < live_ref[0])
            def _():
                back_ref[slots_ref[slot]] = total_ref[:, slot * width:(slot + 1) * width].T.astype(BF16)


def local(features, proj, class_emb, lists, labels):
    blocks = lax.axis_size("cls")
    groups = lax.axis_size("dp")
    own_block = lax.axis_index("cls")
    width = features.shape[0]
    block_width, rank_width = class_emb.shape
    hidden = jnp.dot(features, proj, preferred_element_type=F32).astype(BF16)
    near, far = gather_cls(hidden)

    table = lists[:, 0, :]
    group_labels = labels[:, 0, :]
    block_ids = jnp.arange(blocks, dtype=jnp.int32)
    places = ((block_ids ^ own_block) & 1) * (NX * NY) + block_ids // 2
    listed_by = jnp.any(table == own_block, axis=1)
    list_rank = jnp.cumsum(listed_by.astype(jnp.int32)) - 1
    live = jnp.sum(listed_by.astype(jnp.int32))
    slot_ids = jnp.arange(LIST, dtype=jnp.int32)
    chosen = (list_rank[None, :] == slot_ids[:, None]) & listed_by[None, :]
    slot_places = jnp.sum(jnp.where(chosen, places[None, :], 0), axis=1)
    same = (table[:, :, None, None] == table[None, None]) & (block_ids[None, None, :, None] < block_ids[:, None, None, None])
    entry_rank = jnp.sum(same.astype(jnp.int32), axis=(2, 3))
    entry_place = table * (2 * LIST) + entry_rank
    entry_place = jnp.where(table >= 0, entry_place, -1)
    asked = jnp.concatenate([chosen, (block_ids == own_block)[None]], axis=0)
    queries = jnp.sum(jnp.where(asked[:, :, None], entry_place[None], 0), axis=1).reshape(-1)
    slot_labels = jnp.sum(jnp.where(chosen[:, :, None], group_labels[None], 0), axis=1)
    slot_labels = jnp.where(slot_ids[:, None] < live, slot_labels - own_block * block_width, -1)
    slot_labels = slot_labels.reshape(-1)
    inside = (slot_labels >= 0) & (slot_labels < block_width)
    targets = jnp.take(class_emb, jnp.clip(slot_labels, 0, block_width - 1), axis=0, mode="clip")
    targets = jnp.where(inside[:, None], targets, jnp.zeros((), BF16))
    slot_labels = spread(slot_labels, 8)

    steps = block_width // TILE
    all_rows = LIST * width
    smem = pl.BlockSpec(memory_space=pltpu.SMEM)
    whole = pl.BlockSpec(memory_space=pltpu.VMEM)
    tiled = pl.BlockSpec((TILE, rank_width), lambda i: (i, 0))
    fixed = lambda shape: pl.BlockSpec(shape, lambda i: (0,) * len(shape))
    params = pltpu.CompilerParams(vmem_limit_bytes=48 * 1024 * 1024)
    rows, stats = pl.pallas_call(
        stats_kernel,
        grid=(steps,),
        in_specs=[smem, whole, whole, whole, tiled],
        out_specs=[fixed((all_rows, rank_width)), fixed((2 * LIST, width))],
        out_shape=[jax.ShapeDtypeStruct((all_rows, rank_width), BF16), jax.ShapeDtypeStruct((2 * LIST, width), F32)],
        scratch_shapes=[pltpu.VMEM((8, all_rows), F32)] * 2,
        compiler_params=params,
    )(slot_places, near, far, targets, class_emb)

    all_stats = lax.all_to_all(spread(stats, blocks), "cls", 0, 0, tiled=True)
    class_part, outbox, loss = pl.pallas_call(
        grads_kernel,
        grid=(steps,),
        in_specs=[smem, smem, smem, whole, whole, whole, tiled],
        out_specs=[tiled, fixed((blocks, width, rank_width)), fixed((1, width))],
        out_shape=[
            jax.ShapeDtypeStruct((block_width, rank_width), BF16),
            jax.ShapeDtypeStruct((blocks, width, rank_width), BF16),
            jax.ShapeDtypeStruct((1, width), F32),
        ],
        scratch_shapes=[pltpu.VMEM((8, all_rows), F32), pltpu.VMEM((rank_width, all_rows), F32)],
        compiler_params=params,
    )(slot_places, live.reshape(1), queries, all_stats, slot_labels, rows, class_emb)

    class_grad = lax.psum_scatter(class_part, "dp", scatter_dimension=0, tiled=True).astype(F32)
    row_grad = scatter_cls(outbox.reshape(NK, NX, NY, width, rank_width))
    proj_part = lax.dot_general(features, row_grad, (((0,), (0,)), ((), ())), preferred_element_type=F32)
    share = proj_part.shape[0] // (blocks * groups)
    proj_part = proj_part.reshape(NX * NY, NK, groups * share, rank_width)
    core = own_block % NK
    kept = lax.dynamic_index_in_dim(proj_part, core, 1, keepdims=False)
    given = lax.dynamic_index_in_dim(proj_part, 1 - core, 1, keepdims=False)
    total = kept + lax.ppermute(given, "cls", SWAP_K)
    total = jnp.sum(exchange(total.reshape(NX, NY, groups * share, rank_width), GROUP_X), axis=0)
    total = jnp.sum(exchange(total, GROUP_Y), axis=0)
    total = total.reshape(groups, share, rank_width)
    proj_grad = jnp.sum(lax.all_to_all(total, "dp", 0, 0, tiled=True), axis=0)
    return loss.reshape(-1), class_grad, proj_grad


def solution(mesh):
    in_specs = (
        P(("cls", "dp"), None),
        P(),
        P("cls", None),
        P(None, "dp", None),
        P(None, "dp", None),
    )
    out_specs = (P(("cls", "dp")), P(("cls", "dp"), None), P(("cls", "dp"), None))
    return jax.shard_map(local, mesh=mesh, in_specs=in_specs, out_specs=out_specs, check_vma=False)
```

```python
import jax
import jax.numpy as jnp
from jax import lax
from jax.experimental import pallas as pl
from jax.experimental.pallas import tpu as pltpu
from jax.sharding import PartitionSpec as P

LIST = 6
NX, NY, NK = 4, 8, 2
STATS_TILE = 2048
TILE = 1024
PIECE = 256
NEG = -1e30
F32 = jnp.float32
BF16 = jnp.bfloat16
GROUP_Y = [[x * 16 + y * 2 + k for y in range(NY)] for x in range(NX) for k in range(NK)]
GROUP_X = [[x * 16 + y * 2 + k for x in range(NX)] for y in range(NY) for k in range(NK)]
SWAP_K = [(c, c ^ 1) for c in range(NX * NY * NK)]


def exchange(value, groups):
    return lax.all_to_all(value, "cls", 0, 0, axis_index_groups=groups, tiled=True)


def spread(value, count):
    return jnp.broadcast_to(value[None], (count,) + value.shape)


def gather_cls(block):
    along_y = exchange(spread(block, NY), GROUP_Y)
    own = exchange(spread(along_y, NX), GROUP_X).reshape((NX * NY,) + block.shape)
    return own, lax.ppermute(own, "cls", SWAP_K)


def scatter_cls(outbox):
    swapped = lax.ppermute(outbox[1], "cls", SWAP_K)
    total = (outbox[0].astype(F32) + swapped.astype(F32)).astype(BF16)
    total = jnp.sum(exchange(total, GROUP_X), axis=0, dtype=F32).astype(BF16)
    return jnp.sum(exchange(total, GROUP_Y), axis=0, dtype=F32).astype(BF16)


def scores_of(factors, rows):
    return lax.dot_general(factors, rows, (((1,), (1,)), ((), ())), preferred_element_type=F32)


def stats_kernel(slots_ref, own_ref, other_ref, target_ref, emb_ref, rows_ref, stat_ref, peak_ref, mass_ref):
    step = pl.program_id(0)
    width = rows_ref.shape[0] // LIST

    @pl.when(step == 0)
    def _():
        for slot in range(LIST):
            place = slots_ref[slot]
            near = own_ref[lax.rem(place, NX * NY)]
            far = other_ref[lax.rem(place, NX * NY)]
            rows_ref[slot * width:(slot + 1) * width, :] = jnp.where(place < NX * NY, near, far)
        peak_ref[...] = jnp.full(peak_ref.shape, NEG, F32)
        mass_ref[...] = jnp.zeros(mass_ref.shape, F32)

    for start in range(0, emb_ref.shape[0], PIECE):
        factors = emb_ref[start:start + PIECE, :]
        scores = scores_of(factors, rows_ref[...]).reshape(PIECE // 8, 8, rows_ref.shape[0])
        old = peak_ref[...]
        new = jnp.maximum(old, jnp.max(scores, axis=0))
        mass_ref[...] = mass_ref[...] * jnp.exp(old - new) + jnp.sum(jnp.exp(scores - new[None]), axis=0)
        peak_ref[...] = new

    @pl.when(step == pl.num_programs(0) - 1)
    def _():
        peak = jnp.max(peak_ref[...], axis=0, keepdims=True)
        mass = jnp.sum(mass_ref[...] * jnp.exp(peak_ref[...] - peak), axis=0, keepdims=True)
        norm = peak + jnp.log(mass)
        products = rows_ref[...].astype(F32) * target_ref[...].astype(F32)
        ones = jnp.ones((8, products.shape[1]), F32)
        score = lax.dot_general(ones, products, (((1,), (1,)), ((), ())), precision=lax.Precision.HIGHEST, preferred_element_type=F32)
        for slot in range(LIST):
            stat_ref[slot:slot + 1, :] = norm[:, slot * width:(slot + 1) * width]
            stat_ref[LIST + slot:LIST + 1 + slot, :] = score[0:1, slot * width:(slot + 1) * width]


def grads_kernel(slots_ref, live_ref, query_ref, stat_ref, label_ref, rows_ref, emb_ref, part_ref, back_ref, loss_ref, norm_ref, total_ref):
    step = pl.program_id(0)
    width = rows_ref.shape[0] // LIST

    def combined(which):
        norms, label_score = [], jnp.zeros((1, width), F32)
        for entry in range(LIST):
            place = query_ref[which * LIST + entry]
            base = jnp.maximum(place, 0)
            block, rank = base // (2 * LIST), lax.rem(base, 2 * LIST)
            norm = stat_ref[block, pl.ds(rank, 1), :]
            score = stat_ref[block, pl.ds(rank + LIST, 1), :]
            norms.append(jnp.where(place >= 0, norm, NEG))
            label_score = label_score + jnp.where(place >= 0, score, 0.0)
        peak = norms[0]
        for norm in norms[1:]:
            peak = jnp.maximum(peak, norm)
        mass = jnp.zeros((1, width), F32)
        for norm in norms:
            mass = mass + jnp.exp(norm - peak)
        return peak + jnp.log(mass), label_score

    @pl.when(step == 0)
    def _():
        for slot in range(LIST):
            norm, _ = combined(slot)
            norm_ref[0:1, slot * width:(slot + 1) * width] = jnp.where(slot < live_ref[0], norm, -NEG)
        norm, label_score = combined(LIST)
        loss_ref[...] = norm - label_score
        total_ref[...] = jnp.zeros(total_ref.shape, F32)
        back_ref[...] = jnp.zeros(back_ref.shape, BF16)

    tile = emb_ref.shape[0]
    rows = rows_ref[...]
    class_ids = lax.broadcasted_iota(jnp.int32, (PIECE, rows.shape[0]), 0)
    total = total_ref[...]
    for start in range(0, tile, PIECE):
        factors = emb_ref[start:start + PIECE, :]
        probs = jnp.exp(scores_of(factors, rows) - norm_ref[0:1, :])
        hit = class_ids == label_ref[0:1, :] - (step * tile + start)
        weights = jnp.where(hit, probs - 1.0, probs).astype(BF16)
        part_ref[start:start + PIECE, :] = jnp.dot(weights, rows, preferred_element_type=F32).astype(BF16)
        total = total + lax.dot_general(factors, weights, (((0,), (0,)), ((), ())), preferred_element_type=F32)
    total_ref[...] = total

    @pl.when(step == pl.num_programs(0) - 1)
    def _():
        for slot in range(LIST):
            @pl.when(slot < live_ref[0])
            def _():
                back_ref[slots_ref[slot]] = total_ref[:, slot * width:(slot + 1) * width].T.astype(BF16)


def local(features, proj, class_emb, lists, labels):
    blocks = lax.axis_size("cls")
    groups = lax.axis_size("dp")
    own_block = lax.axis_index("cls")
    width = features.shape[0]
    block_width, rank_width = class_emb.shape
    hidden = jnp.dot(features, proj, preferred_element_type=F32).astype(BF16)
    near, far = gather_cls(hidden)

    table = lists[:, 0, :]
    group_labels = labels[:, 0, :]
    block_ids = jnp.arange(blocks, dtype=jnp.int32)
    places = ((block_ids ^ own_block) & 1) * (NX * NY) + block_ids // 2
    listed_by = jnp.any(table == own_block, axis=1)
    list_rank = jnp.cumsum(listed_by.astype(jnp.int32)) - 1
    live = jnp.sum(listed_by.astype(jnp.int32))
    slot_ids = jnp.arange(LIST, dtype=jnp.int32)
    chosen = (list_rank[None, :] == slot_ids[:, None]) & listed_by[None, :]
    slot_places = jnp.sum(jnp.where(chosen, places[None, :], 0), axis=1)
    same = (table[:, :, None, None] == table[None, None]) & (block_ids[None, None, :, None] < block_ids[:, None, None, None])
    entry_rank = jnp.sum(same.astype(jnp.int32), axis=(2, 3))
    entry_place = table * (2 * LIST) + entry_rank
    entry_place = jnp.where(table >= 0, entry_place, -1)
    asked = jnp.concatenate([chosen, (block_ids == own_block)[None]], axis=0)
    queries = jnp.sum(jnp.where(asked[:, :, None], entry_place[None], 0), axis=1).reshape(-1)
    slot_labels = jnp.sum(jnp.where(chosen[:, :, None], group_labels[None], 0), axis=1)
    slot_labels = jnp.where(slot_ids[:, None] < live, slot_labels - own_block * block_width, -1)
    slot_labels = slot_labels.reshape(-1)
    inside = (slot_labels >= 0) & (slot_labels < block_width)
    targets = jnp.take(class_emb, jnp.clip(slot_labels, 0, block_width - 1), axis=0, mode="clip")
    targets = jnp.where(inside[:, None], targets, jnp.zeros((), BF16))
    slot_labels = spread(slot_labels, 8)

    steps = block_width // TILE
    all_rows = LIST * width
    smem = pl.BlockSpec(memory_space=pltpu.SMEM)
    whole = pl.BlockSpec(memory_space=pltpu.VMEM)
    tiled = pl.BlockSpec((TILE, rank_width), lambda i: (i, 0))
    fixed = lambda shape: pl.BlockSpec(shape, lambda i: (0,) * len(shape))
    params = pltpu.CompilerParams(vmem_limit_bytes=48 * 1024 * 1024)
    rows, stats = pl.pallas_call(
        stats_kernel,
        grid=(block_width // STATS_TILE,),
        in_specs=[smem, whole, whole, whole, pl.BlockSpec((STATS_TILE, rank_width), lambda i: (i, 0))],
        out_specs=[fixed((all_rows, rank_width)), fixed((2 * LIST, width))],
        out_shape=[jax.ShapeDtypeStruct((all_rows, rank_width), BF16), jax.ShapeDtypeStruct((2 * LIST, width), F32)],
        scratch_shapes=[pltpu.VMEM((8, all_rows), F32)] * 2,
        compiler_params=params,
    )(slot_places, near, far, targets, class_emb)

    all_stats = lax.all_to_all(spread(stats, blocks), "cls", 0, 0, tiled=True)
    class_part, outbox, loss = pl.pallas_call(
        grads_kernel,
        grid=(steps,),
        in_specs=[smem, smem, smem, whole, whole, whole, tiled],
        out_specs=[tiled, fixed((blocks, width, rank_width)), fixed((1, width))],
        out_shape=[
            jax.ShapeDtypeStruct((block_width, rank_width), BF16),
            jax.ShapeDtypeStruct((blocks, width, rank_width), BF16),
            jax.ShapeDtypeStruct((1, width), F32),
        ],
        scratch_shapes=[pltpu.VMEM((8, all_rows), F32), pltpu.VMEM((rank_width, all_rows), F32)],
        compiler_params=params,
    )(slot_places, live.reshape(1), queries, all_stats, slot_labels, rows, class_emb)

    class_grad = lax.psum_scatter(class_part, "dp", scatter_dimension=0, tiled=True).astype(F32)
    row_grad = scatter_cls(outbox.reshape(NK, NX, NY, width, rank_width))
    proj_part = lax.dot_general(features, row_grad, (((0,), (0,)), ((), ())), preferred_element_type=F32).astype(BF16)
    share = proj_part.shape[0] // (blocks * groups)
    proj_part = proj_part.reshape(NX * NY, NK, groups * share, rank_width)
    core = own_block % NK
    kept = lax.dynamic_index_in_dim(proj_part, core, 1, keepdims=False)
    given = lax.dynamic_index_in_dim(proj_part, 1 - core, 1, keepdims=False)
    total = (kept.astype(F32) + lax.ppermute(given, "cls", SWAP_K).astype(F32)).astype(BF16)
    total = exchange(total.reshape(NX, NY, groups * share, rank_width), GROUP_X)
    total = exchange(jnp.sum(total, axis=0, dtype=F32).astype(BF16), GROUP_Y)
    total = jnp.sum(total, axis=0, dtype=F32).reshape(groups, share, rank_width)
    proj_grad = jnp.sum(lax.all_to_all(total, "dp", 0, 0, tiled=True), axis=0)
    return loss.reshape(-1), class_grad, proj_grad


def solution(mesh):
    in_specs = (
        P(("cls", "dp"), None),
        P(),
        P("cls", None),
        P(None, "dp", None),
        P(None, "dp", None),
    )
    out_specs = (P(("cls", "dp")), P(("cls", "dp"), None), P(("cls", "dp"), None))
    return jax.shard_map(local, mesh=mesh, in_specs=in_specs, out_specs=out_specs, check_vma=False)
```

```python
import jax
import jax.numpy as jnp
from jax import lax
from jax.experimental import pallas as pl
from jax.experimental.pallas import tpu as pltpu
from jax.sharding import PartitionSpec as P

LIST = 6
NX, NY, NK = 4, 8, 2
STATS_TILE = 2048
TILE = 1024
PIECE = 256
NEG = -1e30
F32 = jnp.float32
BF16 = jnp.bfloat16
GROUP_Y = [[x * 16 + y * 2 + k for y in range(NY)] for x in range(NX) for k in range(NK)]
GROUP_X = [[x * 16 + y * 2 + k for x in range(NX)] for y in range(NY) for k in range(NK)]
SWAP_K = [(c, c ^ 1) for c in range(NX * NY * NK)]


def exchange(value, groups):
    return lax.all_to_all(value, "cls", 0, 0, axis_index_groups=groups, tiled=True)


def spread(value, count):
    return jnp.broadcast_to(value[None], (count,) + value.shape)


def gather_cls(block):
    along_y = exchange(spread(block, NY), GROUP_Y)
    own = exchange(spread(along_y, NX), GROUP_X).reshape((NX * NY,) + block.shape)
    return own, lax.ppermute(own, "cls", SWAP_K)


def scatter_cls(total):
    total = jnp.sum(exchange(total, GROUP_X), axis=0, dtype=F32).astype(BF16)
    return jnp.sum(exchange(total, GROUP_Y), axis=0, dtype=F32).astype(BF16)


def scores_of(factors, rows):
    return lax.dot_general(factors, rows, (((1,), (1,)), ((), ())), preferred_element_type=F32)


def stats_kernel(slots_ref, own_ref, other_ref, target_ref, emb_ref, rows_ref, stat_ref, score_ref, peak_ref, mass_ref):
    step = pl.program_id(0)
    width = rows_ref.shape[0] // LIST

    @pl.when(step == 0)
    def _():
        for slot in range(LIST):
            place = slots_ref[slot]
            near = own_ref[lax.rem(place, NX * NY)]
            far = other_ref[lax.rem(place, NX * NY)]
            rows_ref[slot * width:(slot + 1) * width, :] = jnp.where(place < NX * NY, near, far)
        peak_ref[...] = jnp.full(peak_ref.shape, NEG, F32)
        mass_ref[...] = jnp.zeros(mass_ref.shape, F32)

    for start in range(0, emb_ref.shape[0], PIECE):
        factors = emb_ref[start:start + PIECE, :]
        scores = scores_of(factors, rows_ref[...]).reshape(PIECE // 8, 8, rows_ref.shape[0])
        old = peak_ref[...]
        new = jnp.maximum(old, jnp.max(scores, axis=0))
        mass_ref[...] = mass_ref[...] * jnp.exp(old - new) + jnp.sum(jnp.exp(scores - new[None]), axis=0)
        peak_ref[...] = new

    @pl.when(step == pl.num_programs(0) - 1)
    def _():
        peak = jnp.max(peak_ref[...], axis=0, keepdims=True)
        mass = jnp.sum(mass_ref[...] * jnp.exp(peak_ref[...] - peak), axis=0, keepdims=True)
        norm = peak + jnp.log(mass)
        products = rows_ref[...].astype(F32) * target_ref[...].astype(F32)
        ones = jnp.ones((8, products.shape[1]), F32)
        score = lax.dot_general(ones, products, (((1,), (1,)), ((), ())), precision=lax.Precision.HIGHEST, preferred_element_type=F32)
        stat_ref[...] = jnp.zeros(stat_ref.shape, F32)
        score_ref[...] = jnp.zeros(score_ref.shape, F32)
        for slot in range(LIST):
            stat_ref[slot:slot + 1, :] = norm[:, slot * width:(slot + 1) * width]
            score_ref[slot:slot + 1, :] = score[0:1, slot * width:(slot + 1) * width]


def grads_kernel(live_ref, query_ref, stat_ref, label_ref, rows_ref, emb_ref, part_ref, back_ref, own_ref, norm_ref, total_ref):
    step = pl.program_id(0)
    width = rows_ref.shape[0] // LIST

    def combined(which):
        norms = []
        for entry in range(LIST):
            place = query_ref[which * LIST + entry]
            base = jnp.maximum(place, 0)
            norm = stat_ref[base // 8, pl.ds(lax.rem(base, 8), 1), :]
            norms.append(jnp.where(place >= 0, norm, NEG))
        peak = norms[0]
        for norm in norms[1:]:
            peak = jnp.maximum(peak, norm)
        mass = jnp.zeros((1, width), F32)
        for norm in norms:
            mass = mass + jnp.exp(norm - peak)
        return peak + jnp.log(mass)

    @pl.when(step == 0)
    def _():
        for slot in range(LIST):
            norm = combined(slot)
            norm_ref[0:1, slot * width:(slot + 1) * width] = jnp.where(slot < live_ref[0], norm, -NEG)
        own_ref[...] = combined(LIST)
        total_ref[...] = jnp.zeros(total_ref.shape, F32)

    tile = emb_ref.shape[0]
    rows = rows_ref[...]
    class_ids = lax.broadcasted_iota(jnp.int32, (PIECE, rows.shape[0]), 0)
    total = total_ref[...]
    for start in range(0, tile, PIECE):
        factors = emb_ref[start:start + PIECE, :]
        probs = jnp.exp(scores_of(factors, rows) - norm_ref[0:1, :])
        hit = class_ids == label_ref[0:1, :] - (step * tile + start)
        weights = jnp.where(hit, probs - 1.0, probs).astype(BF16)
        part_ref[start:start + PIECE, :] = jnp.dot(weights, rows, preferred_element_type=F32).astype(BF16)
        total = total + lax.dot_general(factors, weights, (((0,), (0,)), ((), ())), preferred_element_type=F32)
    total_ref[...] = total

    @pl.when(step == pl.num_programs(0) - 1)
    def _():
        for slot in range(LIST):
            back_ref[slot] = total_ref[:, slot * width:(slot + 1) * width].T.astype(BF16)


def place_kernel(own_ref, other_ref, back_ref, arrived_ref, out_ref):
    out_ref[...] = jnp.zeros(out_ref.shape, BF16)
    for slot in range(LIST):
        @pl.when(own_ref[slot] >= 0)
        def _():
            out_ref[own_ref[slot]] = back_ref[slot]
    for slot in range(LIST):
        @pl.when(other_ref[slot] >= 0)
        def _():
            held = out_ref[other_ref[slot]].astype(F32)
            out_ref[other_ref[slot]] = (held + arrived_ref[slot].astype(F32)).astype(BF16)


def local(features, proj, class_emb, lists, labels):
    blocks = lax.axis_size("cls")
    groups = lax.axis_size("dp")
    own_block = lax.axis_index("cls")
    width = features.shape[0]
    block_width, rank_width = class_emb.shape
    hidden = jnp.dot(features, proj, preferred_element_type=F32).astype(BF16)
    near, far = gather_cls(hidden)

    table = lists[:, 0, :]
    group_labels = labels[:, 0, :]
    block_ids = jnp.arange(blocks, dtype=jnp.int32)
    places = ((block_ids ^ own_block) & 1) * (NX * NY) + block_ids // 2
    listed_by = jnp.any(table == own_block, axis=1)
    list_rank = jnp.cumsum(listed_by.astype(jnp.int32)) - 1
    live = jnp.sum(listed_by.astype(jnp.int32))
    slot_ids = jnp.arange(LIST, dtype=jnp.int32)
    chosen = (list_rank[None, :] == slot_ids[:, None]) & listed_by[None, :]
    slot_places = jnp.sum(jnp.where(chosen, places[None, :], 0), axis=1)
    core = own_block % NK

    def kept_places(block):
        listed = jnp.any(table == block, axis=1)
        rank = jnp.cumsum(listed.astype(jnp.int32)) - 1
        taken = (rank[None, :] == slot_ids[:, None]) & (listed & (block_ids % NK == core))[None, :]
        return jnp.sum(jnp.where(taken, block_ids[None, :] // NK + 1, 0), axis=1) - 1

    same = (table[:, :, None, None] == table[None, None]) & (block_ids[None, None, :, None] < block_ids[:, None, None, None])
    entry_rank = jnp.sum(same.astype(jnp.int32), axis=(2, 3))
    entry_place = table * 8 + entry_rank
    entry_place = jnp.where(table >= 0, entry_place, -1)
    asked = jnp.concatenate([chosen, (block_ids == own_block)[None]], axis=0)
    queries = jnp.sum(jnp.where(asked[:, :, None], entry_place[None], 0), axis=1).reshape(-1)
    slot_labels = jnp.sum(jnp.where(chosen[:, :, None], group_labels[None], 0), axis=1)
    slot_labels = jnp.where(slot_ids[:, None] < live, slot_labels - own_block * block_width, -1)
    slot_labels = slot_labels.reshape(-1)
    inside = (slot_labels >= 0) & (slot_labels < block_width)
    targets = jnp.take(class_emb, jnp.clip(slot_labels, 0, block_width - 1), axis=0, mode="clip")
    targets = jnp.where(inside[:, None], targets, jnp.zeros((), BF16))
    slot_labels = spread(slot_labels, 8)

    steps = block_width // TILE
    all_rows = LIST * width
    smem = pl.BlockSpec(memory_space=pltpu.SMEM)
    whole = pl.BlockSpec(memory_space=pltpu.VMEM)
    tiled = pl.BlockSpec((TILE, rank_width), lambda i: (i, 0))
    fixed = lambda shape: pl.BlockSpec(shape, lambda i: (0,) * len(shape))
    params = pltpu.CompilerParams(vmem_limit_bytes=48 * 1024 * 1024)
    rows, stats, scores = pl.pallas_call(
        stats_kernel,
        grid=(block_width // STATS_TILE,),
        in_specs=[smem, whole, whole, whole, pl.BlockSpec((STATS_TILE, rank_width), lambda i: (i, 0))],
        out_specs=[fixed((all_rows, rank_width)), fixed((8, width)), fixed((8, width))],
        out_shape=[jax.ShapeDtypeStruct((all_rows, rank_width), BF16), jax.ShapeDtypeStruct((8, width), F32), jax.ShapeDtypeStruct((8, width), F32)],
        scratch_shapes=[pltpu.VMEM((8, all_rows), F32)] * 2,
        compiler_params=params,
    )(slot_places, near, far, targets, class_emb)

    all_scores = lax.all_gather(scores, "cls")
    all_stats = lax.all_to_all(spread(stats, blocks), "cls", 0, 0, tiled=True)
    class_part, back, own_norm = pl.pallas_call(
        grads_kernel,
        grid=(steps,),
        in_specs=[smem, smem, whole, whole, whole, tiled],
        out_specs=[tiled, fixed((LIST, width, rank_width)), fixed((1, width))],
        out_shape=[
            jax.ShapeDtypeStruct((block_width, rank_width), BF16),
            jax.ShapeDtypeStruct((LIST, width, rank_width), BF16),
            jax.ShapeDtypeStruct((1, width), F32),
        ],
        scratch_shapes=[pltpu.VMEM((8, all_rows), F32), pltpu.VMEM((rank_width, all_rows), F32)],
        compiler_params=params,
    )(live.reshape(1), queries, all_stats, slot_labels, rows, class_emb)

    class_grad = lax.psum_scatter(class_part, "dp", scatter_dimension=0, tiled=True).astype(F32)
    merged = pl.pallas_call(
        place_kernel,
        in_specs=[smem, smem, whole, whole],
        out_specs=whole,
        out_shape=jax.ShapeDtypeStruct((NX * NY, width, rank_width), BF16),
        compiler_params=params,
    )(kept_places(own_block), kept_places(own_block ^ 1), back, lax.ppermute(back, "cls", SWAP_K))
    row_grad = scatter_cls(merged.reshape(NX, NY, width, rank_width))
    proj_part = lax.dot_general(features, row_grad, (((0,), (0,)), ((), ())), preferred_element_type=F32).astype(BF16)
    share = proj_part.shape[0] // (blocks * groups)
    proj_part = proj_part.reshape(NX * NY, NK, groups * share, rank_width)
    kept = lax.dynamic_index_in_dim(proj_part, core, 1, keepdims=False)
    given = lax.dynamic_index_in_dim(proj_part, 1 - core, 1, keepdims=False)
    total = (kept.astype(F32) + lax.ppermute(given, "cls", SWAP_K).astype(F32)).astype(BF16)
    total = exchange(total.reshape(NX, NY, groups * share, rank_width), GROUP_X)
    total = exchange(jnp.sum(total, axis=0, dtype=F32).astype(BF16), GROUP_Y)
    total = jnp.sum(total, axis=0, dtype=F32).reshape(groups, share, rank_width)
    proj_grad = jnp.sum(lax.all_to_all(total, "dp", 0, 0, tiled=True), axis=0)
    own_places = queries[LIST * LIST:]
    spots = jnp.arange(blocks * 8, dtype=jnp.int32)
    wanted = jnp.any(spots[:, None] == own_places[None, :], axis=1)
    label_score = jnp.sum(jnp.where(wanted[:, None], all_scores.reshape(blocks * 8, width), 0.0), axis=0)
    return own_norm.reshape(-1) - label_score, class_grad, proj_grad


def solution(mesh):
    in_specs = (
        P(("cls", "dp"), None),
        P(),
        P("cls", None),
        P(None, "dp", None),
        P(None, "dp", None),
    )
    out_specs = (P(("cls", "dp")), P(("cls", "dp"), None), P(("cls", "dp"), None))
    return jax.shard_map(local, mesh=mesh, in_specs=in_specs, out_specs=out_specs, check_vma=False)
```

```python
import jax
import jax.numpy as jnp
from jax import lax
from jax.experimental import pallas as pl
from jax.experimental.pallas import tpu as pltpu
from jax.sharding import PartitionSpec as P

LIST = 6
NX, NY, NK = 4, 8, 2
STATS_TILE = 2048
TILE = 1024
PIECE = 256
EXTRA = 16
NEG = -1e30
F32 = jnp.float32
BF16 = jnp.bfloat16
GROUP_Y = [[x * 16 + y * 2 + k for y in range(NY)] for x in range(NX) for k in range(NK)]
GROUP_X = [[x * 16 + y * 2 + k for x in range(NX)] for y in range(NY) for k in range(NK)]
SWAP_K = [(c, c ^ 1) for c in range(NX * NY * NK)]


def exchange(value, groups):
    return lax.all_to_all(value, "cls", 0, 0, axis_index_groups=groups, tiled=True)


def spread(value, count):
    return jnp.broadcast_to(value[None], (count,) + value.shape)


def gather_cls(block):
    along_y = exchange(spread(block, NY), GROUP_Y)
    own = exchange(spread(along_y, NX), GROUP_X).reshape((NX * NY,) + block.shape)
    return own, lax.ppermute(own, "cls", SWAP_K)


def scatter_cls(total):
    total = jnp.sum(exchange(total, GROUP_X), axis=0, dtype=F32).astype(BF16)
    return jnp.sum(exchange(total, GROUP_Y), axis=0, dtype=F32).astype(BF16)


def scores_of(factors, rows):
    return lax.dot_general(factors, rows, (((1,), (1,)), ((), ())), preferred_element_type=F32)


def stats_kernel(slots_ref, own_ref, other_ref, target_ref, emb_ref, rows_ref, stat_ref, score_ref, peak_ref, mass_ref):
    step = pl.program_id(0)
    width = rows_ref.shape[0] // LIST

    @pl.when(step == 0)
    def _():
        for slot in range(LIST):
            place = slots_ref[slot]
            near = own_ref[lax.rem(place, NX * NY)]
            far = other_ref[lax.rem(place, NX * NY)]
            rows_ref[slot * width:(slot + 1) * width, :] = jnp.where(place < NX * NY, near, far)
        peak_ref[...] = jnp.full(peak_ref.shape, NEG, F32)
        mass_ref[...] = jnp.zeros(mass_ref.shape, F32)

    for start in range(0, emb_ref.shape[0], PIECE):
        factors = emb_ref[start:start + PIECE, :]
        scores = scores_of(factors, rows_ref[...]).reshape(PIECE // 8, 8, rows_ref.shape[0])
        old = peak_ref[...]
        new = jnp.maximum(old, jnp.max(scores, axis=0))
        mass_ref[...] = mass_ref[...] * jnp.exp(old - new) + jnp.sum(jnp.exp(scores - new[None]), axis=0)
        peak_ref[...] = new

    @pl.when(step == pl.num_programs(0) - 1)
    def _():
        peak = jnp.max(peak_ref[...], axis=0, keepdims=True)
        mass = jnp.sum(mass_ref[...] * jnp.exp(peak_ref[...] - peak), axis=0, keepdims=True)
        norm = peak + jnp.log(mass)
        products = rows_ref[...].astype(F32) * target_ref[...].astype(F32)
        ones = jnp.ones((8, products.shape[1]), F32)
        score = lax.dot_general(ones, products, (((1,), (1,)), ((), ())), precision=lax.Precision.HIGHEST, preferred_element_type=F32)
        stat_ref[...] = jnp.zeros(stat_ref.shape, F32)
        score_ref[...] = jnp.zeros(score_ref.shape, F32)
        for slot in range(LIST):
            stat_ref[slot:slot + 1, :] = norm[:, slot * width:(slot + 1) * width]
            score_ref[slot:slot + 1, :] = score[0:1, slot * width:(slot + 1) * width]


def grads_kernel(live_ref, query_ref, stat_ref, score_ref, label_ref, rows_ref, emb_ref, part_ref, back_ref, own_ref, norm_ref, total_ref):
    step = pl.program_id(0)
    width = rows_ref.shape[0] // LIST

    def combined(which):
        norms = []
        for entry in range(LIST):
            place = query_ref[which * LIST + entry]
            base = jnp.maximum(place, 0)
            norm = stat_ref[base // 8, pl.ds(lax.rem(base, 8), 1), :]
            norms.append(jnp.where(place >= 0, norm, NEG))
        peak = norms[0]
        for norm in norms[1:]:
            peak = jnp.maximum(peak, norm)
        mass = jnp.zeros((1, width), F32)
        for norm in norms:
            mass = mass + jnp.exp(norm - peak)
        return peak + jnp.log(mass)

    @pl.when(step == 0)
    def _():
        for slot in range(LIST):
            norm = combined(slot)
            norm_ref[0:1, slot * width:(slot + 1) * width] = jnp.where(slot < live_ref[0], norm, -NEG)
        own_ref[...] = combined(LIST)
        total_ref[...] = jnp.zeros(total_ref.shape, F32)

    tile = emb_ref.shape[0]
    rows = rows_ref[...]
    class_ids = lax.broadcasted_iota(jnp.int32, (PIECE, rows.shape[0]), 0)
    total = total_ref[...]
    for start in range(0, tile, PIECE):
        factors = emb_ref[start:start + PIECE, :]
        probs = jnp.exp(scores_of(factors, rows) - norm_ref[0:1, :])
        hit = class_ids == label_ref[0:1, :] - (step * tile + start)
        weights = jnp.where(hit, probs - 1.0, probs).astype(BF16)
        part_ref[start:start + PIECE, :] = jnp.dot(weights, rows, preferred_element_type=F32).astype(BF16)
        total = total + lax.dot_general(factors, weights, (((0,), (0,)), ((), ())), preferred_element_type=F32)
    total_ref[...] = total

    @pl.when(step == pl.num_programs(0) - 1)
    def _():
        for slot in range(LIST):
            back_ref[slot, 0:width, :] = total_ref[:, slot * width:(slot + 1) * width].T.astype(BF16)
            score = score_ref[slot:slot + 1, :]
            high = score.astype(BF16).astype(F32)
            middle = (score - high).astype(BF16).astype(F32)
            low = score - high - middle
            line = lax.broadcasted_iota(jnp.int32, (EXTRA, width), 0)
            parts = jnp.where(line == 0, high, jnp.where(line == 1, middle, jnp.where(line == 2, low, 0.0)))
            back_ref[slot, width:width + EXTRA, :] = parts.astype(BF16)


def place_kernel(own_ref, other_ref, back_ref, arrived_ref, out_ref):
    out_ref[...] = jnp.zeros(out_ref.shape, BF16)
    for slot in range(LIST):
        @pl.when(own_ref[slot] >= 0)
        def _():
            out_ref[own_ref[slot]] = back_ref[slot]
    for slot in range(LIST):
        @pl.when(other_ref[slot] >= 0)
        def _():
            held = out_ref[other_ref[slot]].astype(F32)
            out_ref[other_ref[slot]] = (held + arrived_ref[slot].astype(F32)).astype(BF16)


def local(features, proj, class_emb, lists, labels):
    blocks = lax.axis_size("cls")
    groups = lax.axis_size("dp")
    own_block = lax.axis_index("cls")
    width = features.shape[0]
    block_width, rank_width = class_emb.shape
    hidden = jnp.dot(features, proj, preferred_element_type=F32).astype(BF16)
    near, far = gather_cls(hidden)

    table = lists[:, 0, :]
    group_labels = labels[:, 0, :]
    block_ids = jnp.arange(blocks, dtype=jnp.int32)
    places = ((block_ids ^ own_block) & 1) * (NX * NY) + block_ids // 2
    listed_by = jnp.any(table == own_block, axis=1)
    list_rank = jnp.cumsum(listed_by.astype(jnp.int32)) - 1
    live = jnp.sum(listed_by.astype(jnp.int32))
    slot_ids = jnp.arange(LIST, dtype=jnp.int32)
    chosen = (list_rank[None, :] == slot_ids[:, None]) & listed_by[None, :]
    slot_places = jnp.sum(jnp.where(chosen, places[None, :], 0), axis=1)
    core = own_block % NK

    def kept_places(block):
        listed = jnp.any(table == block, axis=1)
        rank = jnp.cumsum(listed.astype(jnp.int32)) - 1
        taken = (rank[None, :] == slot_ids[:, None]) & (listed & (block_ids % NK == core))[None, :]
        return jnp.sum(jnp.where(taken, block_ids[None, :] // NK + 1, 0), axis=1) - 1

    same = (table[:, :, None, None] == table[None, None]) & (block_ids[None, None, :, None] < block_ids[:, None, None, None])
    entry_rank = jnp.sum(same.astype(jnp.int32), axis=(2, 3))
    entry_place = table * 8 + entry_rank
    entry_place = jnp.where(table >= 0, entry_place, -1)
    asked = jnp.concatenate([chosen, (block_ids == own_block)[None]], axis=0)
    queries = jnp.sum(jnp.where(asked[:, :, None], entry_place[None], 0), axis=1).reshape(-1)
    slot_labels = jnp.sum(jnp.where(chosen[:, :, None], group_labels[None], 0), axis=1)
    slot_labels = jnp.where(slot_ids[:, None] < live, slot_labels - own_block * block_width, -1)
    slot_labels = slot_labels.reshape(-1)
    inside = (slot_labels >= 0) & (slot_labels < block_width)
    targets = jnp.take(class_emb, jnp.clip(slot_labels, 0, block_width - 1), axis=0, mode="clip")
    targets = jnp.where(inside[:, None], targets, jnp.zeros((), BF16))
    slot_labels = spread(slot_labels, 8)

    steps = block_width // TILE
    all_rows = LIST * width
    smem = pl.BlockSpec(memory_space=pltpu.SMEM)
    whole = pl.BlockSpec(memory_space=pltpu.VMEM)
    tiled = pl.BlockSpec((TILE, rank_width), lambda i: (i, 0))
    fixed = lambda shape: pl.BlockSpec(shape, lambda i: (0,) * len(shape))
    params = pltpu.CompilerParams(vmem_limit_bytes=48 * 1024 * 1024)
    rows, stats, scores = pl.pallas_call(
        stats_kernel,
        grid=(block_width // STATS_TILE,),
        in_specs=[smem, whole, whole, whole, pl.BlockSpec((STATS_TILE, rank_width), lambda i: (i, 0))],
        out_specs=[fixed((all_rows, rank_width)), fixed((8, width)), fixed((8, width))],
        out_shape=[jax.ShapeDtypeStruct((all_rows, rank_width), BF16), jax.ShapeDtypeStruct((8, width), F32), jax.ShapeDtypeStruct((8, width), F32)],
        scratch_shapes=[pltpu.VMEM((8, all_rows), F32)] * 2,
        compiler_params=params,
    )(slot_places, near, far, targets, class_emb)

    all_stats = lax.all_to_all(spread(stats, blocks), "cls", 0, 0, tiled=True)
    class_part, back, own_norm = pl.pallas_call(
        grads_kernel,
        grid=(steps,),
        in_specs=[smem, smem, whole, whole, whole, whole, tiled],
        out_specs=[tiled, fixed((LIST, width + EXTRA, rank_width)), fixed((1, width))],
        out_shape=[
            jax.ShapeDtypeStruct((block_width, rank_width), BF16),
            jax.ShapeDtypeStruct((LIST, width + EXTRA, rank_width), BF16),
            jax.ShapeDtypeStruct((1, width), F32),
        ],
        scratch_shapes=[pltpu.VMEM((8, all_rows), F32), pltpu.VMEM((rank_width, all_rows), F32)],
        compiler_params=params,
    )(live.reshape(1), queries, all_stats, scores, slot_labels, rows, class_emb)

    class_grad = lax.psum_scatter(class_part, "dp", scatter_dimension=0, tiled=True).astype(F32)
    merged = pl.pallas_call(
        place_kernel,
        in_specs=[smem, smem, whole, whole],
        out_specs=whole,
        out_shape=jax.ShapeDtypeStruct((NX * NY, width + EXTRA, rank_width), BF16),
        compiler_params=params,
    )(kept_places(own_block), kept_places(own_block ^ 1), back, lax.ppermute(back, "cls", SWAP_K))
    summed = scatter_cls(merged.reshape(NX, NY, width + EXTRA, rank_width))
    row_grad = summed[:width]
    label_score = jnp.sum(summed[width:width + 3].astype(F32), axis=0)
    proj_part = lax.dot_general(features, row_grad, (((0,), (0,)), ((), ())), preferred_element_type=F32).astype(BF16)
    share = proj_part.shape[0] // (blocks * groups)
    proj_part = proj_part.reshape(NX * NY, NK, groups * share, rank_width)
    kept = lax.dynamic_index_in_dim(proj_part, core, 1, keepdims=False)
    given = lax.dynamic_index_in_dim(proj_part, 1 - core, 1, keepdims=False)
    total = (kept.astype(F32) + lax.ppermute(given, "cls", SWAP_K).astype(F32)).astype(BF16)
    total = exchange(total.reshape(NX, NY, groups * share, rank_width), GROUP_X)
    total = exchange(jnp.sum(total, axis=0, dtype=F32).astype(BF16), GROUP_Y)
    total = jnp.sum(total, axis=0, dtype=F32).reshape(groups, share, rank_width)
    proj_grad = jnp.sum(lax.all_to_all(total, "dp", 0, 0, tiled=True), axis=0)
    return own_norm.reshape(-1) - label_score, class_grad, proj_grad


def solution(mesh):
    in_specs = (
        P(("cls", "dp"), None),
        P(),
        P("cls", None),
        P(None, "dp", None),
        P(None, "dp", None),
    )
    out_specs = (P(("cls", "dp")), P(("cls", "dp"), None), P(("cls", "dp"), None))
    return jax.shard_map(local, mesh=mesh, in_specs=in_specs, out_specs=out_specs, check_vma=False)
```

```python
import jax
import jax.numpy as jnp
from jax import lax
from jax.experimental import pallas as pl
from jax.experimental.pallas import tpu as pltpu
from jax.sharding import PartitionSpec as P

LIST = 6
NX, NY, NK = 4, 8, 2
STATS_TILE = 4096
TILE = 1024
PIECE = 256
EXTRA = 16
NEG = -1e30
F32 = jnp.float32
BF16 = jnp.bfloat16
GROUP_Y = [[x * 16 + y * 2 + k for y in range(NY)] for x in range(NX) for k in range(NK)]
GROUP_X = [[x * 16 + y * 2 + k for x in range(NX)] for y in range(NY) for k in range(NK)]
SWAP_K = [(c, c ^ 1) for c in range(NX * NY * NK)]


def exchange(value, groups):
    return lax.all_to_all(value, "cls", 0, 0, axis_index_groups=groups, tiled=True)


def spread(value, count):
    return jnp.broadcast_to(value[None], (count,) + value.shape)


def gather_cls(block):
    along_y = exchange(spread(block, NY), GROUP_Y)
    own = exchange(spread(along_y, NX), GROUP_X).reshape((NX * NY,) + block.shape)
    return own, lax.ppermute(own, "cls", SWAP_K)


def scatter_cls(total):
    total = jnp.sum(exchange(total, GROUP_X), axis=0, dtype=F32).astype(BF16)
    return jnp.sum(exchange(total, GROUP_Y), axis=0, dtype=F32).astype(BF16)


def scores_of(factors, rows):
    return lax.dot_general(factors, rows, (((1,), (1,)), ((), ())), preferred_element_type=F32)


def stats_kernel(slots_ref, own_ref, other_ref, target_ref, emb_ref, rows_ref, stat_ref, score_ref, peak_ref, mass_ref):
    step = pl.program_id(0)
    width = rows_ref.shape[0] // LIST

    @pl.when(step == 0)
    def _():
        for slot in range(LIST):
            place = slots_ref[slot]
            near = own_ref[lax.rem(place, NX * NY)]
            far = other_ref[lax.rem(place, NX * NY)]
            rows_ref[slot * width:(slot + 1) * width, :] = jnp.where(place < NX * NY, near, far)
        peak_ref[...] = jnp.full(peak_ref.shape, NEG, F32)
        mass_ref[...] = jnp.zeros(mass_ref.shape, F32)

    for start in range(0, emb_ref.shape[0], PIECE):
        factors = emb_ref[start:start + PIECE, :]
        scores = scores_of(factors, rows_ref[...]).reshape(PIECE // 8, 8, rows_ref.shape[0])
        old = peak_ref[...]
        new = jnp.maximum(old, jnp.max(scores, axis=0))
        mass_ref[...] = mass_ref[...] * jnp.exp(old - new) + jnp.sum(jnp.exp(scores - new[None]), axis=0)
        peak_ref[...] = new

    @pl.when(step == pl.num_programs(0) - 1)
    def _():
        peak = jnp.max(peak_ref[...], axis=0, keepdims=True)
        mass = jnp.sum(mass_ref[...] * jnp.exp(peak_ref[...] - peak), axis=0, keepdims=True)
        norm = peak + jnp.log(mass)
        products = rows_ref[...].astype(F32) * target_ref[...].astype(F32)
        ones = jnp.ones((8, products.shape[1]), F32)
        score = lax.dot_general(ones, products, (((1,), (1,)), ((), ())), precision=lax.Precision.HIGHEST, preferred_element_type=F32)
        stat_ref[...] = jnp.zeros(stat_ref.shape, F32)
        score_ref[...] = jnp.zeros(score_ref.shape, F32)
        for slot in range(LIST):
            stat_ref[slot:slot + 1, :] = norm[:, slot * width:(slot + 1) * width]
            score_ref[slot:slot + 1, :] = score[0:1, slot * width:(slot + 1) * width]


def grads_kernel(live_ref, query_ref, stat_ref, score_ref, label_ref, rows_ref, emb_ref, part_ref, back_ref, own_ref, norm_ref, total_ref):
    step = pl.program_id(0)
    width = rows_ref.shape[0] // LIST

    def combined(which):
        norms = []
        for entry in range(LIST):
            place = query_ref[which * LIST + entry]
            base = jnp.maximum(place, 0)
            norm = stat_ref[base // 8, pl.ds(lax.rem(base, 8), 1), :]
            norms.append(jnp.where(place >= 0, norm, NEG))
        peak = norms[0]
        for norm in norms[1:]:
            peak = jnp.maximum(peak, norm)
        mass = jnp.zeros((1, width), F32)
        for norm in norms:
            mass = mass + jnp.exp(norm - peak)
        return peak + jnp.log(mass)

    @pl.when(step == 0)
    def _():
        for slot in range(LIST):
            norm = combined(slot)
            norm_ref[0:1, slot * width:(slot + 1) * width] = jnp.where(slot < live_ref[0], norm, -NEG)
        own_ref[...] = combined(LIST)
        total_ref[...] = jnp.zeros(total_ref.shape, F32)

    tile = emb_ref.shape[0]
    rows = rows_ref[...]
    class_ids = lax.broadcasted_iota(jnp.int32, (PIECE, rows.shape[0]), 0)
    total = total_ref[...]
    for start in range(0, tile, PIECE):
        factors = emb_ref[start:start + PIECE, :]
        probs = jnp.exp(scores_of(factors, rows) - norm_ref[0:1, :])
        hit = class_ids == label_ref[0:1, :] - (step * tile + start)
        weights = jnp.where(hit, probs - 1.0, probs).astype(BF16)
        part_ref[start:start + PIECE, :] = jnp.dot(weights, rows, preferred_element_type=F32).astype(BF16)
        total = total + lax.dot_general(factors, weights, (((0,), (0,)), ((), ())), preferred_element_type=F32)
    total_ref[...] = total

    @pl.when(step == pl.num_programs(0) - 1)
    def _():
        for slot in range(LIST):
            back_ref[slot, 0:width, :] = total_ref[:, slot * width:(slot + 1) * width].T.astype(BF16)
            score = score_ref[slot:slot + 1, :]
            high = score.astype(BF16).astype(F32)
            middle = (score - high).astype(BF16).astype(F32)
            low = score - high - middle
            line = lax.broadcasted_iota(jnp.int32, (EXTRA, width), 0)
            parts = jnp.where(line == 0, high, jnp.where(line == 1, middle, jnp.where(line == 2, low, 0.0)))
            back_ref[slot, width:width + EXTRA, :] = parts.astype(BF16)


def place_kernel(own_ref, other_ref, back_ref, arrived_ref, out_ref):
    out_ref[...] = jnp.zeros(out_ref.shape, BF16)
    for slot in range(LIST):
        @pl.when(own_ref[slot] >= 0)
        def _():
            out_ref[own_ref[slot]] = back_ref[slot]
    for slot in range(LIST):
        @pl.when(other_ref[slot] >= 0)
        def _():
            held = out_ref[other_ref[slot]].astype(F32)
            out_ref[other_ref[slot]] = (held + arrived_ref[slot].astype(F32)).astype(BF16)


def local(features, proj, class_emb, lists, labels):
    blocks = lax.axis_size("cls")
    groups = lax.axis_size("dp")
    own_block = lax.axis_index("cls")
    width = features.shape[0]
    block_width, rank_width = class_emb.shape
    hidden = jnp.dot(features, proj, preferred_element_type=F32).astype(BF16)
    near, far = gather_cls(hidden)

    table = lists[:, 0, :]
    group_labels = labels[:, 0, :]
    block_ids = jnp.arange(blocks, dtype=jnp.int32)
    places = ((block_ids ^ own_block) & 1) * (NX * NY) + block_ids // 2
    listed_by = jnp.any(table == own_block, axis=1)
    list_rank = jnp.cumsum(listed_by.astype(jnp.int32)) - 1
    live = jnp.sum(listed_by.astype(jnp.int32))
    slot_ids = jnp.arange(LIST, dtype=jnp.int32)
    chosen = (list_rank[None, :] == slot_ids[:, None]) & listed_by[None, :]
    slot_places = jnp.sum(jnp.where(chosen, places[None, :], 0), axis=1)
    core = own_block % NK

    def kept_places(block):
        listed = jnp.any(table == block, axis=1)
        rank = jnp.cumsum(listed.astype(jnp.int32)) - 1
        taken = (rank[None, :] == slot_ids[:, None]) & (listed & (block_ids % NK == core))[None, :]
        return jnp.sum(jnp.where(taken, block_ids[None, :] // NK + 1, 0), axis=1) - 1

    same = (table[:, :, None, None] == table[None, None]) & (block_ids[None, None, :, None] < block_ids[:, None, None, None])
    entry_rank = jnp.sum(same.astype(jnp.int32), axis=(2, 3))
    entry_place = table * 8 + entry_rank
    entry_place = jnp.where(table >= 0, entry_place, -1)
    asked = jnp.concatenate([chosen, (block_ids == own_block)[None]], axis=0)
    queries = jnp.sum(jnp.where(asked[:, :, None], entry_place[None], 0), axis=1).reshape(-1)
    slot_labels = jnp.sum(jnp.where(chosen[:, :, None], group_labels[None], 0), axis=1)
    slot_labels = jnp.where(slot_ids[:, None] < live, slot_labels - own_block * block_width, -1)
    slot_labels = slot_labels.reshape(-1)
    inside = (slot_labels >= 0) & (slot_labels < block_width)
    targets = jnp.take(class_emb, jnp.clip(slot_labels, 0, block_width - 1), axis=0, mode="clip")
    targets = jnp.where(inside[:, None], targets, jnp.zeros((), BF16))
    slot_labels = spread(slot_labels, 8)

    steps = block_width // TILE
    all_rows = LIST * width
    smem = pl.BlockSpec(memory_space=pltpu.SMEM)
    whole = pl.BlockSpec(memory_space=pltpu.VMEM)
    tiled = pl.BlockSpec((TILE, rank_width), lambda i: (i, 0))
    fixed = lambda shape: pl.BlockSpec(shape, lambda i: (0,) * len(shape))
    params = pltpu.CompilerParams(vmem_limit_bytes=48 * 1024 * 1024)
    rows, stats, scores = pl.pallas_call(
        stats_kernel,
        grid=(block_width // STATS_TILE,),
        in_specs=[smem, whole, whole, whole, pl.BlockSpec((STATS_TILE, rank_width), lambda i: (i, 0))],
        out_specs=[fixed((all_rows, rank_width)), fixed((8, width)), fixed((8, width))],
        out_shape=[jax.ShapeDtypeStruct((all_rows, rank_width), BF16), jax.ShapeDtypeStruct((8, width), F32), jax.ShapeDtypeStruct((8, width), F32)],
        scratch_shapes=[pltpu.VMEM((8, all_rows), F32)] * 2,
        compiler_params=params,
    )(slot_places, near, far, targets, class_emb)

    all_stats = lax.all_to_all(spread(stats, blocks), "cls", 0, 0, tiled=True)
    class_part, back, own_norm = pl.pallas_call(
        grads_kernel,
        grid=(steps,),
        in_specs=[smem, smem, whole, whole, whole, whole, tiled],
        out_specs=[tiled, fixed((LIST, width + EXTRA, rank_width)), fixed((1, width))],
        out_shape=[
            jax.ShapeDtypeStruct((block_width, rank_width), BF16),
            jax.ShapeDtypeStruct((LIST, width + EXTRA, rank_width), BF16),
            jax.ShapeDtypeStruct((1, width), F32),
        ],
        scratch_shapes=[pltpu.VMEM((8, all_rows), F32), pltpu.VMEM((rank_width, all_rows), F32)],
        compiler_params=params,
    )(live.reshape(1), queries, all_stats, scores, slot_labels, rows, class_emb)

    class_grad = lax.psum_scatter(class_part, "dp", scatter_dimension=0, tiled=True).astype(F32)
    merged = pl.pallas_call(
        place_kernel,
        in_specs=[smem, smem, whole, whole],
        out_specs=whole,
        out_shape=jax.ShapeDtypeStruct((NX * NY, width + EXTRA, rank_width), BF16),
        compiler_params=params,
    )(kept_places(own_block), kept_places(own_block ^ 1), back, lax.ppermute(back, "cls", SWAP_K))
    summed = scatter_cls(merged.reshape(NX, NY, width + EXTRA, rank_width))
    row_grad = summed[:width]
    label_score = jnp.sum(summed[width:width + 3].astype(F32), axis=0)
    proj_part = lax.dot_general(features, row_grad, (((0,), (0,)), ((), ())), preferred_element_type=F32).astype(BF16)
    share = proj_part.shape[0] // (blocks * groups)
    proj_part = proj_part.reshape(NX * NY, NK, groups * share, rank_width)
    kept = lax.dynamic_index_in_dim(proj_part, core, 1, keepdims=False)
    given = lax.dynamic_index_in_dim(proj_part, 1 - core, 1, keepdims=False)
    total = (kept.astype(F32) + lax.ppermute(given, "cls", SWAP_K).astype(F32)).astype(BF16)
    total = exchange(total.reshape(NX, NY, groups * share, rank_width), GROUP_X)
    total = exchange(jnp.sum(total, axis=0, dtype=F32).astype(BF16), GROUP_Y)
    total = jnp.sum(total, axis=0, dtype=F32).reshape(groups, share, rank_width)
    proj_grad = jnp.sum(lax.all_to_all(total, "dp", 0, 0, tiled=True), axis=0)
    return own_norm.reshape(-1) - label_score, class_grad, proj_grad


def solution(mesh):
    in_specs = (
        P(("cls", "dp"), None),
        P(),
        P("cls", None),
        P(None, "dp", None),
        P(None, "dp", None),
    )
    out_specs = (P(("cls", "dp")), P(("cls", "dp"), None), P(("cls", "dp"), None))
    return jax.shard_map(local, mesh=mesh, in_specs=in_specs, out_specs=out_specs, check_vma=False)
```
